32 devices in a mesh: row: 4 (over y, x), col: 8 (over z, core).
Axes of the slice: x: 2, y: 2, z: 4, core: 2. Of those that a mesh axis runs over, the one named last changes fastest.
Arguments:
- front_trailing: float32 [16384, 16384], P('row', 'col'), may hold values from -6 to 6
- panel_columns: float32 [16384, 1024], P('row', 'col'), may hold values from -0.1875 to 0.1875
- panel_rows: float32 [1024, 16384], P('row', 'col'), may hold values from -6 to 6
- pivots: int32 [1024], replicated, may hold values from 0 to 1023, each once
- diag_inverse: float32 [1024, 1024], replicated, may hold values from -0.1875 to 0.1875
- test_matrix: float32 [16384, 512], P('col'), may hold values from -0.046875 to 0.046875
Outputs:
- schur: float32 [16384, 16384], P('row', 'col')
- off_samples: float32 [16384, 512], P(('row', 'col'))
- leaf_blocks: float32 [16384, 128], P(('row', 'col'))
- group_gram: float32 [4, 512, 512], P('row')
The draws below stay inside these ranges and needn't reach their ends.
Inputs may be any that keep to these rules, and one draw needn't show every extreme that they name: pivots names each of 0 to 1023 once.
All inputs are finite; a program needn't handle non-finite values.
Results may differ from the reference program's by a relative error of at most 0.000084.
Values sent between devices are 32-bit elements; how exact they have to be, the bound alone decides.
No kernel may reach another device: no remote copies, remote signals or barrier semaphores. Data moves between devices by JAX's collectives and lax.ppermute only.
A program may use at most 192 MiB of HBM per device.

```python
import jax
import jax.numpy as jnp
from jax import lax

ORDER = 16384
PANEL = 1024
SAMPLES = 512
LEAF = 128
GROUP_ROWS = 8192
N_ROW = 4


def levels(rng, shape, shards, smallest, high):
    level, own = 1.0, jax.random.fold_in(rng, 6)
    for axis_at, blocks in shards:
        steps = jnp.exp(jax.random.uniform(jax.random.fold_in(own, axis_at), (blocks,), jnp.float32, smallest / len(shards), high / len(shards)))
        level = level * jnp.repeat(steps, shape[axis_at] // blocks).reshape([-1 if axis == axis_at else 1 for axis in range(len(shape))])
    return level


def scatter_about(stream_key, dims, spread, reach, pieces=(), kind=jnp.bfloat16):
    drawn = jax.random.normal(stream_key, dims, jnp.float32) * spread
    if len(pieces) > 0:
        drawn = levels(stream_key, dims, pieces, -0.22, 0.18) * drawn
    return jnp.clip(drawn, min=-reach, max=reach).astype(kind)


def setup_inputs(seed: int = 0) -> dict:
    arg_keys = jax.random.split(jax.random.key(seed), 7)
    front_trailing = scatter_about(arg_keys[0], (ORDER, ORDER), 1.0, 6.0, ((0, 4), (1, 8)), jnp.float32)
    panel_columns = scatter_about(arg_keys[1], (ORDER, PANEL), PANEL ** -0.5, 0.1875, ((0, 4), (1, 8)), jnp.float32)
    panel_rows = scatter_about(arg_keys[2], (PANEL, ORDER), 1.0, 6.0, ((0, 4), (1, 8)), jnp.float32)
    pivots = jax.random.permutation(arg_keys[3], PANEL).astype(jnp.int32)
    diag_inverse = scatter_about(arg_keys[4], (PANEL, PANEL), PANEL ** -0.5, 0.1875, (), jnp.float32)
    test_matrix = scatter_about(arg_keys[5], (ORDER, SAMPLES), ORDER ** -0.5, 0.046875, ((0, 8),), jnp.float32)
    return dict(front_trailing=front_trailing, panel_columns=panel_columns, panel_rows=panel_rows, pivots=pivots, diag_inverse=diag_inverse, test_matrix=test_matrix)


def reference(front_trailing, panel_columns, panel_rows, pivots, diag_inverse, test_matrix):
    highest = lax.Precision.HIGHEST
    upper = jnp.take(panel_rows, pivots, axis=0)
    lower = jnp.dot(panel_columns, diag_inverse, precision=highest, preferred_element_type=jnp.float32)
    schur = front_trailing - jnp.dot(lower, upper, precision=highest, preferred_element_type=jnp.float32)
    leaf_ids = jnp.arange(ORDER, dtype=jnp.int32) // LEAF
    masked = jnp.where(leaf_ids[:, None] == leaf_ids[None, :], jnp.zeros_like(schur), schur)
    off_samples = jnp.dot(masked, test_matrix, precision=highest, preferred_element_type=jnp.float32)
    count = ORDER // LEAF
    blocks = jnp.diagonal(schur.reshape(count, LEAF, count, LEAF), axis1=0, axis2=2)
    leaf_blocks = jnp.moveaxis(blocks, -1, 0).reshape(ORDER, LEAF)
    groups = off_samples.reshape(N_ROW // 2, GROUP_ROWS, SAMPLES)
    gram = jnp.einsum("gri,grj->gij", groups, groups, precision=highest) / GROUP_ROWS
    group_gram = jnp.repeat(gram, 2, axis=0)
    return (schur, off_samples, leaf_blocks, group_gram)
```

```python
import functools

import jax
import jax.numpy as jnp
from jax import lax
from jax.experimental import pallas as pl
from jax.experimental.pallas import tpu as pltpu
from jax.sharding import Mesh, PartitionSpec as P

LEAF = 128
CHUNKS = 4
VMEM = 56 * 1024 * 1024
F32 = jnp.float32
BF16 = jnp.bfloat16
ALL = ("hi", "lo", "z", "core")


def split(value):
    high = value.astype(BF16)
    return high, (value - high.astype(F32)).astype(BF16)


def split_outside(value):
    high = lax.reduce_precision(value, exponent_bits=8, mantissa_bits=7)
    return high.astype(BF16), (value - high).astype(BF16)


def triple(left_high, left_low, right_high, right_low):
    dot = functools.partial(jnp.dot, preferred_element_type=F32)
    return dot(left_high, right_high) + (dot(left_high, right_low) + dot(left_low, right_high))


def high_dot(left, right, dims=(((1,), (0,)), ((), ()))):
    return lax.dot_general(left, right, dims, precision=lax.Precision.HIGH, preferred_element_type=F32)


def swap(value, axis):
    return lax.ppermute(value, axis, [(0, 1), (1, 0)])


def shift(value, axis, step):
    count = lax.axis_size(axis)
    return lax.ppermute(value, axis, [(at, (at + step) % count) for at in range(count)])


def hop(value, step, count=None):
    chips = lax.axis_size("z")
    count = chips - 1 if count is None else count
    if step > 0:
        route = [(at, at + 1) for at in range(count)]
    else:
        route = [(at, at - 1) for at in range(chips - count, chips)]
    return lax.ppermute(value, "z", route)


def samples_kernel(place, front, test, out, test_high, test_low):
    step = pl.program_id(0)

    @pl.when(step == 0)
    def _():
        high, low = split(test[...])
        test_high[...] = high
        test_low[...] = low

    rows, width = front.shape
    first_row = place[1] + (2 * step + place[0]) * (rows // LEAF)
    row_leaf = first_row + lax.broadcasted_iota(jnp.int32, (rows, 1), 0) // LEAF
    col_leaf = place[2] + lax.broadcasted_iota(jnp.int32, (1, width), 1) // LEAF
    value = jnp.where(row_leaf == col_leaf, 0.0, front[...])
    high, low = split(value)
    out[...] = triple(high, low, test_high[...], test_low[...])


def samples_half(front, test, place, rows):
    height, width = front.shape
    samples = test.shape[1]
    tiles = height // (2 * rows)
    flops = 6 * tiles * rows * width * samples
    return pl.pallas_call(
        samples_kernel,
        out_shape=jax.ShapeDtypeStruct((tiles * rows, samples), F32),
        grid_spec=pltpu.PrefetchScalarGridSpec(
            num_scalar_prefetch=1,
            grid=(tiles,),
            in_specs=[
                pl.BlockSpec((rows, width), lambda s, place: (2 * s + place[0], 0)),
                pl.BlockSpec((width, samples), lambda s, place: (0, 0), pipeline_mode=pl.Buffered(1)),
            ],
            out_specs=pl.BlockSpec((rows, samples), lambda s, place: (s, 0)),
            scratch_shapes=[pltpu.VMEM((width, samples), BF16)] * 2,
        ),
        compiler_params=pltpu.CompilerParams(vmem_limit_bytes=VMEM),
        cost_estimate=pl.CostEstimate(flops=flops, bytes_accessed=height * width * 2, transcendentals=0),
        name="samples",
    )(place, front, test)


def weights_kernel(parts, *refs):
    left_high, left_low = refs[0], refs[1]
    rows = jnp.concatenate([ref[...] for ref in refs[2 : 2 + parts]], axis=0)
    high, low = split(rows)
    out_high, out_low = refs[2 + parts :]
    high, low = split(triple(left_high[...], left_low[...], high, low))
    out_high[...] = high
    out_low[...] = low


def weights(left_high, left_low, blocks):
    panel = left_high.shape[0]
    width = blocks[0].shape[1]
    tile = min(width, 512)
    whole = pl.BlockSpec((panel, panel), lambda n: (0, 0), pipeline_mode=pl.Buffered(1))
    return pl.pallas_call(
        functools.partial(weights_kernel, len(blocks)),
        out_shape=[jax.ShapeDtypeStruct((panel, width), BF16)] * 2,
        grid=(width // tile,),
        in_specs=[whole, whole] + [pl.BlockSpec((b.shape[0], tile), lambda n: (0, n)) for b in blocks],
        out_specs=[pl.BlockSpec((panel, tile), lambda n: (0, n))] * 2,
        compiler_params=pltpu.CompilerParams(vmem_limit_bytes=VMEM),
        cost_estimate=pl.CostEstimate(flops=6 * panel * panel * width, bytes_accessed=panel * width * 8, transcendentals=0),
        name="weights",
    )(left_high, left_low, *blocks)


def update_kernel(first, place, own, beside, mine, other, high, low, front, *refs):
    out, leaves = refs[-2:]
    columns = jnp.concatenate([own[...], beside[...], mine[...], other[...]], axis=1)
    left_high, left_low = split(columns)
    out[...] = front[...] - triple(left_high, left_low, high[...], low[...])
    rows, width = out.shape
    leaf = place[1] - place[2] + first + pl.program_id(0) * (rows // LEAF)
    for at in range(rows // LEAF):
        column = jnp.clip(leaf + at, 0, width // LEAF - 1) * LEAF
        piece = pl.ds(at * LEAF, LEAF)
        leaves[piece, :] = out[piece, pl.ds(pl.multiple_of(column, LEAF), LEAF)]


def update(place, own, beside, mine, other, high, low, front, schur, start):
    height, width = front.shape
    panel = high.shape[0]
    rows = mine.shape[0]
    tile = 256 if rows % 256 == 0 else LEAF
    base = start // tile
    slot = own.shape[1]
    far = mine.shape[1]
    whole = pl.BlockSpec((panel, width), lambda i, place: (0, 0), pipeline_mode=pl.Buffered(1))
    operands = [place, own, beside, mine, other, high, low, front]
    specs = [
        pl.BlockSpec((tile, slot), lambda i, place: (base + i, 0)),
        pl.BlockSpec((tile, slot), lambda i, place: (base + i, 0)),
        pl.BlockSpec((tile, far), lambda i, place: (i, 0)),
        pl.BlockSpec((tile, far), lambda i, place: (i, 0)),
        whole,
        whole,
        pl.BlockSpec((tile, width), lambda i, place: (base + i, 0)),
    ]
    aliases = {}
    if schur is not None:
        aliases = {len(operands): 0}
        operands.append(schur)
        specs.append(pl.BlockSpec(memory_space=pl.ANY))
    return pl.pallas_call(
        functools.partial(update_kernel, start // LEAF),
        out_shape=[jax.ShapeDtypeStruct((height, width), F32), jax.ShapeDtypeStruct((rows, LEAF), F32)],
        grid_spec=pltpu.PrefetchScalarGridSpec(
            num_scalar_prefetch=1,
            grid=(rows // tile,),
            in_specs=specs,
            out_specs=[
                pl.BlockSpec((tile, width), lambda i, place: (base + i, 0)),
                pl.BlockSpec((tile, LEAF), lambda i, place: (i, 0)),
            ],
        ),
        input_output_aliases=aliases,
        compiler_params=pltpu.CompilerParams(vmem_limit_bytes=VMEM),
        cost_estimate=pl.CostEstimate(
            flops=6 * rows * panel * width, bytes_accessed=rows * width * 8 + panel * width * 4, transcendentals=0
        ),
        name="update",
    )(*operands)


def body(front_trailing, panel_columns, panel_rows, pivots, diag_inverse, test_matrix):
    hi_count, z_count = lax.axis_size("hi"), lax.axis_size("z")
    row_count, col_count = 2 * hi_count, 2 * z_count
    hi, lo, z, core = [lax.axis_index(name) for name in ALL]
    row, col = hi * 2 + lo, z * 2 + core
    height, width = front_trailing.shape
    depth, slot = panel_rows.shape[0], panel_columns.shape[1]
    panel = depth * row_count
    samples = test_matrix.shape[1]
    per = height // col_count
    ratio = col_count // row_count
    targets = col_count // ratio
    chunk = height // CHUNKS
    starts = list(range(0, height, chunk))

    over_lo = swap(panel_rows, "lo")
    over_hi = [shift(panel_rows, "hi", step) for step in range(1, hi_count)]
    blocks, owners = [panel_rows, over_lo], [row, row ^ 1]
    for step, block in enumerate(over_hi, 1):
        far_hi = (hi - step) % hi_count
        first = shift(over_lo[: depth // 2], "hi", step)
        second = swap(block[depth // 2 :], "lo")
        blocks += [block, first, second]
        owners += [far_hi * 2 + lo, far_hi * 2 + (1 - lo)]

    beside = swap(panel_columns, "core")
    gathered = []
    for start in starts:
        right = left = panel_columns[start : start + chunk]
        rights, lefts = [], []
        for _ in range(z_count - 1):
            right, left = hop(right, 1), hop(left, -1)
            rights.append(right)
            lefts.append(left)
        mine = jnp.concatenate(
            [jnp.where(z >= at, rights[at - 1], lefts[z_count - at - 1]) for at in range(1, z_count)], axis=1
        )
        gathered.append((mine, swap(mine, "core")))

    chips = [(z - at) % z_count for at in range(z_count)]
    order = [2 * chips[0] + core, 2 * chips[0] + 1 - core]
    order += [2 * chip + core for chip in chips[1:]] + [2 * chip + 1 - core for chip in chips[1:]]
    left = jnp.take(diag_inverse.reshape(col_count, slot, panel), jnp.stack(order), axis=0).reshape(panel, panel)
    position = (jnp.stack(owners)[:, None] * depth + jnp.arange(depth, dtype=jnp.int32)[None, :]).reshape(panel)
    chosen = (pivots[:, None] == position[None, :]).astype(BF16)
    left_high, left_low = [
        jnp.dot(part, chosen, preferred_element_type=F32).astype(BF16) for part in split_outside(left)
    ]

    inner = lax.psum(high_dot(panel_rows, test_matrix), ("z", "core"))
    inner = lax.all_gather(inner, ("hi", "lo"), axis=0, tiled=False)
    inner = jnp.take(inner, jnp.stack(owners), axis=0).reshape(panel, samples)
    inner_high, inner_low = split_outside(inner)
    near = 2 * slot
    middle = triple(left_high[:near], left_low[:near], inner_high, inner_low)

    row_leaf, col_leaf = row * (height // LEAF), col * (width // LEAF)
    sent = samples_half(front_trailing, test_matrix, jnp.stack([1 - core, row_leaf, col_leaf]), per)
    kept = samples_half(front_trailing, test_matrix, jnp.stack([core, row_leaf, col_leaf]), per)
    sent = swap(sent, "core")
    near_columns = jnp.concatenate([panel_columns, beside], axis=1).reshape(z_count, 2, per, near)
    near_columns = lax.dynamic_index_in_dim(near_columns, core, 1, keepdims=False).reshape(z_count * per, near)
    partial = (kept + sent - high_dot(near_columns, middle)).reshape(z_count, per, samples)
    right = left = None
    for step in range(1, z_count):
        right_part = lax.dynamic_index_in_dim(partial, jnp.minimum(z + z_count - step, z_count - 1), 0, keepdims=False)
        left_part = lax.dynamic_index_in_dim(partial, jnp.maximum(z - z_count + step, 0), 0, keepdims=False)
        right = hop(right_part if right is None else right_part + right, 1, step)
        left = hop(left_part if left is None else left_part + left, -1, step)
    sums = lax.dynamic_index_in_dim(partial, z, 0, keepdims=False) + right + left

    half = col % ratio
    leaf_count = per // LEAF
    routes = [
        [(r * col_count + ratio * r + h, r * col_count + h * targets + m) for r in range(row_count) for h in range(ratio)]
        for m in range(targets)
    ]

    def to_owners(pieces):
        return sum(lax.ppermute(piece, ALL, route) for piece, route in zip(pieces, routes))

    def front_leaf(at):
        return lax.dynamic_slice(front_trailing, (half * width + at * LEAF, at * LEAF), (LEAF, LEAF))

    early = []
    for m in range(targets):
        leaf = jnp.concatenate([front_leaf(m * leaf_count + at) for at in range(leaf_count)], axis=0)
        early.append(jnp.concatenate([test_matrix[m * per : (m + 1) * per], leaf], axis=1))
    early = to_owners(early)
    own_test, own_front = early[:, :samples], early[:, samples:]

    high, low = weights(left_high, left_low, blocks)
    place = jnp.stack([core, row_leaf, col_leaf])
    schur, leaves = None, []
    for start, (mine, other) in zip(starts, gathered):
        schur, leaf = update(place, panel_columns, beside, mine, other, high, low, front_trailing, schur, start)
        leaves.append(leaf)

    def leaf_rows(start):
        return leaves[start // chunk][start % chunk : start % chunk + per]

    late = []
    for m in range(targets):
        piece = leaf_rows(m * per)
        for h in range(1, ratio):
            piece = jnp.where(half == h, leaf_rows(h * width + m * per), piece)
        late.append(piece)
    leaf_blocks = to_owners(late)
    change = (own_front - leaf_blocks).reshape(leaf_count, LEAF, LEAF)
    change = high_dot(change, own_test.reshape(leaf_count, LEAF, samples), (((2,), (1,)), ((0,), (0,))))
    off_samples = sums + change.reshape(per, samples)
    gram = high_dot(off_samples, off_samples, (((0,), (0,)), ((), ())))
    group_gram = (lax.psum(gram, ("lo", "z", "core")) / (2 * height))[None]
    return (schur, off_samples, leaf_blocks, group_gram)


def solution(mesh):
    rows, cols = mesh.shape["row"], mesh.shape["col"]
    fine = Mesh(mesh.devices.reshape(rows // 2, 2, cols // 2, 2), ALL)
    row, col = ("hi", "lo"), ("z", "core")
    placed = (P(row, col), P(row, col), P(row, col), P(), P(), P(col, None))
    return jax.shard_map(
        body,
        mesh=fine,
        in_specs=placed,
        out_specs=(P(row, col), P(ALL, None), P(ALL, None), P(row, None, None)),
        check_vma=False,
    )
```

```python
import functools

import jax
import jax.numpy as jnp
from jax import lax
from jax.experimental import pallas as pl
from jax.experimental.pallas import tpu as pltpu
from jax.sharding import Mesh, PartitionSpec as P

LEAF = 128
SHARES = (8, 5, 3)
VMEM = 56 * 1024 * 1024
F32 = jnp.float32
BF16 = jnp.bfloat16
ALL = ("hi", "lo", "z", "core")


def split(value):
    high = value.astype(BF16)
    return high, (value - high.astype(F32)).astype(BF16)


def split_outside(value):
    high = lax.reduce_precision(value, exponent_bits=8, mantissa_bits=7)
    return high.astype(BF16), (value - high).astype(BF16)


def triple(left_high, left_low, right_high, right_low):
    dot = functools.partial(jnp.dot, preferred_element_type=F32)
    return dot(left_high, right_high) + (dot(left_high, right_low) + dot(left_low, right_high))


def high_dot(left, right, dims=(((1,), (0,)), ((), ()))):
    return lax.dot_general(left, right, dims, precision=lax.Precision.HIGH, preferred_element_type=F32)


def swap(value, axis):
    return lax.ppermute(value, axis, [(0, 1), (1, 0)])


def shift(value, axis, step):
    count = lax.axis_size(axis)
    return lax.ppermute(value, axis, [(at, (at + step) % count) for at in range(count)])


def hop(value, step, count=None):
    chips = lax.axis_size("z")
    count = chips - 1 if count is None else count
    if step > 0:
        route = [(at, at + 1) for at in range(count)]
    else:
        route = [(at, at - 1) for at in range(chips - count, chips)]
    return lax.ppermute(value, "z", route)


def weights_kernel(parts, *refs):
    left_high, left_low = refs[0], refs[1]
    rows = jnp.concatenate([ref[...] for ref in refs[2 : 2 + parts]], axis=0)
    high, low = split(rows)
    out_high, out_low = refs[2 + parts :]
    out_high[...], out_low[...] = split(triple(left_high[...], left_low[...], high, low))


def weights(left_high, left_low, blocks):
    panel = left_high.shape[0]
    width = blocks[0].shape[1]
    tile = min(width, 512)
    whole = pl.BlockSpec((panel, panel), lambda n: (0, 0), pipeline_mode=pl.Buffered(1))
    return pl.pallas_call(
        functools.partial(weights_kernel, len(blocks)),
        out_shape=[jax.ShapeDtypeStruct((panel, width), BF16)] * 2,
        grid=(width // tile,),
        in_specs=[whole, whole] + [pl.BlockSpec((b.shape[0], tile), lambda n: (0, n)) for b in blocks],
        out_specs=[pl.BlockSpec((panel, tile), lambda n: (0, n))] * 2,
        compiler_params=pltpu.CompilerParams(vmem_limit_bytes=VMEM),
        cost_estimate=pl.CostEstimate(flops=6 * panel * panel * width, bytes_accessed=panel * width * 8, transcendentals=0),
        name="weights",
    )(left_high, left_low, *blocks)


def update_kernel(first, place, gathered, beside, high, low, test_high, test_low, front, *refs):
    out, leaves, kept, sent = refs[-4:]
    chips, _, rows, _ = gathered.shape
    width, samples = out.shape[-1], kept.shape[-1]
    per_leaf = place[3]
    columns = [gathered[at].reshape(2 * rows, -1) for at in range(chips)]
    columns += [beside[at].reshape(2 * rows, -1) for at in range(chips)]
    left_high, left_low = split(jnp.concatenate(columns, axis=1))
    dot = functools.partial(jnp.dot, preferred_element_type=F32)

    number = lax.broadcasted_iota(jnp.int32, (2 * rows, 1), 0)
    second = number >= rows
    owner = place[1] + 2 * pl.program_id(0) * per_leaf
    row_leaf = owner + jnp.where(second, per_leaf + (number - rows + first) // LEAF, (number + first) // LEAF)

    step = min(width, 512)
    sums = jnp.zeros((2 * rows, samples), F32)
    for at in range(0, width, step):
        part = slice(at, at + step)
        value = dot(left_high, high[:, part])
        value = value + dot(left_high, low[:, part])
        value = value + dot(left_low, high[:, part])
        value = front[:, :, part].reshape(2 * rows, step) - value
        out[:, :, part] = value.reshape(2, rows, step)
        col_leaf = place[2] + at // LEAF + lax.broadcasted_iota(jnp.int32, (1, step), 1) // LEAF
        value_high, value_low = split(jnp.where(row_leaf == col_leaf, 0.0, value))
        sums = sums + dot(value_high, test_high[part])
        sums = sums + dot(value_high, test_low[part])
        sums = sums + dot(value_low, test_high[part])
    kept[0] = jnp.where(place[0] == 0, sums[:rows], sums[rows:])
    sent[0] = jnp.where(place[0] == 0, sums[rows:], sums[:rows])

    for which in range(2):
        at = 0
        while at < rows:
            size = min(rows - at, LEAF - (first + at) % LEAF)
            leaf = owner + which * per_leaf + (first + at) // LEAF - place[2]
            column = pl.multiple_of(jnp.clip(leaf, 0, width // LEAF - 1) * LEAF, LEAF)
            leaves[which, at : at + size] = out[which, at : at + size, pl.ds(column, LEAF)]
            at += size


def update(place, gathered, beside, weight, test, front, schur, first):
    chips, owners, rows, slot = gathered.shape
    _, per, width = front.shape
    panel, samples = weight[0].shape[0], test[0].shape[1]

    def whole(array):
        return pl.BlockSpec(array.shape, lambda i, place: (0, 0), pipeline_mode=pl.Buffered(1))

    def window(size):
        return pl.BlockSpec(
            (pl.Element(2), pl.Element(rows), pl.Element(size)), lambda i, place: (2 * i, first, 0)
        )

    block = pl.BlockSpec((chips, 2, rows, slot), lambda i, place: (0, i, 0, 0))
    operands = [place, gathered, beside, *weight, *test, front]
    specs = [block, block, *map(whole, weight), *map(whole, test), window(width)]
    aliases = {}
    if schur is not None:
        aliases = {len(operands): 0}
        operands.append(schur)
        specs.append(pl.BlockSpec(memory_space=pl.ANY))
    sums = jax.ShapeDtypeStruct((owners // 2, rows, samples), F32)
    flops = 6 * owners * rows * width * (panel + samples)
    return pl.pallas_call(
        functools.partial(update_kernel, first),
        out_shape=[
            jax.ShapeDtypeStruct(front.shape, F32),
            jax.ShapeDtypeStruct((owners, rows, LEAF), F32),
            sums,
            sums,
        ],
        grid_spec=pltpu.PrefetchScalarGridSpec(
            num_scalar_prefetch=1,
            grid=(owners // 2,),
            in_specs=specs,
            out_specs=[
                window(width),
                pl.BlockSpec((2, rows, LEAF), lambda i, place: (i, 0, 0)),
                pl.BlockSpec((1, rows, samples), lambda i, place: (i, 0, 0)),
                pl.BlockSpec((1, rows, samples), lambda i, place: (i, 0, 0)),
            ],
        ),
        input_output_aliases=aliases,
        compiler_params=pltpu.CompilerParams(vmem_limit_bytes=VMEM),
        cost_estimate=pl.CostEstimate(
            flops=flops, bytes_accessed=owners * rows * width * 8 + panel * width * 4, transcendentals=0
        ),
        name="update",
    )(*operands)


def scatter_sum(kept, sent):
    chips, z = lax.axis_size("z"), lax.axis_index("z")
    partial = kept + swap(sent, "core")
    right = left = None
    for step in range(1, chips):
        right_part = lax.dynamic_index_in_dim(partial, jnp.minimum(z + chips - step, chips - 1), 0, keepdims=False)
        left_part = lax.dynamic_index_in_dim(partial, jnp.maximum(z - chips + step, 0), 0, keepdims=False)
        right = hop(right_part if right is None else right_part + right, 1, step)
        left = hop(left_part if left is None else left_part + left, -1, step)
    return lax.dynamic_index_in_dim(partial, z, 0, keepdims=False) + right + left


def halve(value, axis):
    half = value.shape[0] // 2
    at = lax.axis_index(axis)
    mine = lax.dynamic_slice_in_dim(value, at * half, half, 0)
    return mine + swap(lax.dynamic_slice_in_dim(value, (1 - at) * half, half, 0), axis)


def double(value, axis):
    other = swap(value, axis)
    first = lax.axis_index(axis) == 0
    return jnp.concatenate([jnp.where(first, value, other), jnp.where(first, other, value)], axis=0)


def group_sum(gram):
    chips, z = lax.axis_size("z"), lax.axis_index("z")
    value = halve(halve(gram, "core"), "lo")
    parts = value.reshape(chips, value.shape[0] // chips, value.shape[1])
    total = lax.dynamic_index_in_dim(parts, z, 0, keepdims=False)
    for step in range(1, chips):
        part = lax.dynamic_index_in_dim(parts, (z + step) % chips, 0, keepdims=False)
        total = total + shift(part, "z", step)
    parts = jnp.stack([total] + [shift(total, "z", step) for step in range(1, chips)])
    value = jnp.take(parts, (z - jnp.arange(chips)) % chips, axis=0).reshape(value.shape)
    return double(double(value, "lo"), "core")


def body(front_trailing, panel_columns, panel_rows, pivots, diag_inverse, test_matrix):
    hi_count, z_count = lax.axis_size("hi"), lax.axis_size("z")
    row_count, col_count = 2 * hi_count, 2 * z_count
    hi, lo, z, core = [lax.axis_index(name) for name in ALL]
    row, col = hi * 2 + lo, z * 2 + core
    height, width = front_trailing.shape
    depth, slot = panel_rows.shape[0], panel_columns.shape[1]
    panel = depth * row_count
    samples = test_matrix.shape[1]
    per = height // col_count
    ratio = col_count // row_count
    targets = col_count // ratio

    stops = [per * sum(SHARES[: at + 1]) // 16 for at in range(len(SHARES))]
    chunks = list(zip([0] + stops[:-1], stops))
    owned = panel_columns.reshape(col_count, per, slot)
    gathered = [lax.all_gather(owned[:, start:stop], "z", axis=0, tiled=False) for start, stop in chunks]

    over_lo = swap(panel_rows, "lo")
    over_hi = [shift(panel_rows, "hi", step) for step in range(1, hi_count)]
    blocks, owners = [panel_rows, over_lo], [row, row ^ 1]
    for step, block in enumerate(over_hi, 1):
        far_hi = (hi - step) % hi_count
        first = shift(over_lo[: depth // 2], "hi", step)
        second = swap(block[depth // 2 :], "lo")
        blocks += [block, first, second]
        owners += [far_hi * 2 + lo, far_hi * 2 + (1 - lo)]

    order = [2 * chip + core for chip in range(z_count)] + [2 * chip + 1 - core for chip in range(z_count)]
    left = jnp.take(diag_inverse.reshape(col_count, slot, panel), jnp.stack(order), axis=0).reshape(panel, panel)
    position = (jnp.stack(owners)[:, None] * depth + jnp.arange(depth, dtype=jnp.int32)[None, :]).reshape(panel)
    chosen = (pivots[:, None] == position[None, :]).astype(BF16)
    left_high, left_low = [
        jnp.dot(part, chosen, preferred_element_type=F32).astype(BF16) for part in split_outside(left)
    ]
    weight = weights(left_high, left_low, blocks)
    test = split_outside(test_matrix)

    place = jnp.stack([core, row * (height // LEAF), col * (width // LEAF), jnp.int32(per // LEAF)])
    front = front_trailing.reshape(col_count, per, width)
    schur, leaves, sums = None, [], []
    for (start, stop), mine in zip(chunks, gathered):
        schur, leaf, kept, sent = update(place, mine, swap(mine, "core"), weight, test, front, schur, start)
        leaves.append(leaf)
        sums.append(scatter_sum(kept, sent))

    off_samples = jnp.concatenate(sums, axis=0)
    gram = high_dot(off_samples, off_samples, (((0,), (0,)), ((), ())))
    group_gram = (group_sum(gram) / (2 * height))[None]

    half = col % ratio
    leaf_blocks = 0
    for m in range(targets):
        pieces = [lax.dynamic_index_in_dim(leaf, half * targets + m, 0, keepdims=False) for leaf in leaves]
        route = [
            (r * col_count + ratio * r + h, r * col_count + h * targets + m)
            for r in range(row_count)
            for h in range(ratio)
        ]
        leaf_blocks = leaf_blocks + lax.ppermute(jnp.concatenate(pieces, axis=0), ALL, route)
    return (schur.reshape(height, width), off_samples, leaf_blocks, group_gram)


def solution(mesh):
    rows, cols = mesh.shape["row"], mesh.shape["col"]
    fine = Mesh(mesh.devices.reshape(rows // 2, 2, cols // 2, 2), ALL)
    row, col = ("hi", "lo"), ("z", "core")
    placed = (P(row, col), P(row, col), P(row, col), P(), P(), P(col, None))
    return jax.shard_map(
        body,
        mesh=fine,
        in_specs=placed,
        out_specs=(P(row, col), P(ALL, None), P(ALL, None), P(row, None, None)),
        check_vma=False,
    )
```

```python
import functools

import jax
import jax.numpy as jnp
from jax import lax
from jax.experimental import pallas as pl
from jax.experimental.pallas import tpu as pltpu
from jax.sharding import Mesh, PartitionSpec as P

LEAF = 128
CHUNKS = 4
VMEM = 56 * 1024 * 1024
F32 = jnp.float32
BF16 = jnp.bfloat16
ALL = ("hi", "lo", "z", "core")


def split(value):
    high = value.astype(BF16)
    return high, (value - high.astype(F32)).astype(BF16)


def split_outside(value):
    high = lax.reduce_precision(value, exponent_bits=8, mantissa_bits=7)
    return high.astype(BF16), (value - high).astype(BF16)


def triple(left_high, left_low, right_high, right_low):
    dot = functools.partial(jnp.dot, preferred_element_type=F32)
    return dot(left_high, right_high) + (dot(left_high, right_low) + dot(left_low, right_high))


def high_dot(left, right, dims=(((1,), (0,)), ((), ()))):
    return lax.dot_general(left, right, dims, precision=lax.Precision.HIGH, preferred_element_type=F32)


def swap(value, axis):
    return lax.ppermute(value, axis, [(0, 1), (1, 0)])


def shift(value, axis, step):
    count = lax.axis_size(axis)
    return lax.ppermute(value, axis, [(at, (at + step) % count) for at in range(count)])


def after(value, *others):
    return lax.optimization_barrier((value, others))[0]


def hop(value, step, count=None):
    chips = lax.axis_size("z")
    count = chips - 1 if count is None else count
    if step > 0:
        route = [(at, at + 1) for at in range(count)]
    else:
        route = [(at, at - 1) for at in range(chips - count, chips)]
    return lax.ppermute(value, "z", route)


def samples_kernel(base, place, front, test_high, test_low, *refs):
    out = refs[-1]
    rows, width = front.shape
    first_row = place[1] + (2 * (pl.program_id(0) + base) + place[0]) * (rows // LEAF)
    row_leaf = first_row + lax.broadcasted_iota(jnp.int32, (rows, 1), 0) // LEAF
    step = min(width, 512)
    sums = jnp.zeros(out.shape, F32)
    for at in range(0, width, step):
        part = slice(at, at + step)
        col_leaf = place[2] + at // LEAF + lax.broadcasted_iota(jnp.int32, (1, step), 1) // LEAF
        high, low = split(jnp.where(row_leaf == col_leaf, 0.0, front[:, part]))
        sums = sums + jnp.dot(high, test_high[part], preferred_element_type=F32)
        sums = sums + jnp.dot(high, test_low[part], preferred_element_type=F32)
        sums = sums + jnp.dot(low, test_high[part], preferred_element_type=F32)
    out[...] = sums


def samples_part(front, test, place, rows, base, tiles, total, previous):
    height, width = front.shape
    samples = test[0].shape[1]
    whole = pl.BlockSpec((width, samples), lambda s, place: (0, 0), pipeline_mode=pl.Buffered(1))
    operands = [place, front, *test]
    specs = [pl.BlockSpec((rows, width), lambda s, place: (2 * (s + base) + place[0], 0)), whole, whole]
    aliases = {}
    if previous is not None:
        aliases = {len(operands): 0}
        operands.append(previous)
        specs.append(pl.BlockSpec(memory_space=pl.ANY))
    return pl.pallas_call(
        functools.partial(samples_kernel, base),
        out_shape=jax.ShapeDtypeStruct((total * rows, samples), F32),
        grid_spec=pltpu.PrefetchScalarGridSpec(
            num_scalar_prefetch=1,
            grid=(tiles,),
            in_specs=specs,
            out_specs=pl.BlockSpec((rows, samples), lambda s, place: (s + base, 0)),
        ),
        input_output_aliases=aliases,
        compiler_params=pltpu.CompilerParams(vmem_limit_bytes=VMEM),
        cost_estimate=pl.CostEstimate(
            flops=6 * tiles * rows * width * samples, bytes_accessed=tiles * rows * width * 4, transcendentals=0
        ),
        name="samples",
    )(*operands)


def weights_kernel(parts, *refs):
    left_high, left_low = refs[0], refs[1]
    rows = jnp.concatenate([ref[...] for ref in refs[2 : 2 + parts]], axis=0)
    high, low = split(rows)
    out_high, out_low = refs[2 + parts :]
    out_high[...], out_low[...] = split(triple(left_high[...], left_low[...], high, low))


def weights(left_high, left_low, blocks):
    panel = left_high.shape[0]
    width = blocks[0].shape[1]
    tile = min(width, 512)
    whole = pl.BlockSpec((panel, panel), lambda n: (0, 0), pipeline_mode=pl.Buffered(1))
    return pl.pallas_call(
        functools.partial(weights_kernel, len(blocks)),
        out_shape=[jax.ShapeDtypeStruct((panel, width), BF16)] * 2,
        grid=(width // tile,),
        in_specs=[whole, whole] + [pl.BlockSpec((b.shape[0], tile), lambda n: (0, n)) for b in blocks],
        out_specs=[pl.BlockSpec((panel, tile), lambda n: (0, n))] * 2,
        compiler_params=pltpu.CompilerParams(vmem_limit_bytes=VMEM),
        cost_estimate=pl.CostEstimate(flops=6 * panel * panel * width, bytes_accessed=panel * width * 8, transcendentals=0),
        name="weights",
    )(left_high, left_low, *blocks)


def update_kernel(first, place, own, beside, mine, other, high_all, low_all, front, *refs):
    out, leaves, high, low, sems = refs[-5:]
    rows, width = out.shape
    step = min(width, 512)
    begin = pl.program_id(0) == 0

    def fetches(at):
        part = slice(at, at + step)
        return [
            pltpu.make_async_copy(source.at[:, part], target.at[:, part], sems.at[which, at // step])
            for which, (source, target) in enumerate([(high_all, high), (low_all, low)])
        ]

    @pl.when(begin)
    def _():
        for at in range(0, width, step):
            for fetch in fetches(at):
                fetch.start()

    left_high, left_low = split(jnp.concatenate([own[...], beside[...], mine[...], other[...]], axis=1))
    for at in range(0, width, step):

        @pl.when(begin)
        def _():
            for fetch in fetches(at):
                fetch.wait()

        part = slice(at, at + step)
        value = jnp.dot(left_high, high[:, part], preferred_element_type=F32)
        value = value + jnp.dot(left_high, low[:, part], preferred_element_type=F32)
        value = value + jnp.dot(left_low, high[:, part], preferred_element_type=F32)
        out[:, part] = front[:, part] - value
    leaf = place[1] - place[2] + first + pl.program_id(0) * (rows // LEAF)
    for at in range(rows // LEAF):
        column = jnp.clip(leaf + at, 0, width // LEAF - 1) * LEAF
        piece = pl.ds(at * LEAF, LEAF)
        leaves[piece, :] = out[piece, pl.ds(pl.multiple_of(column, LEAF), LEAF)]


def update(place, own, beside, mine, other, weight, front, schur, start):
    height, width = front.shape
    panel = weight[0].shape[0]
    rows = mine.shape[0]
    tile = 512 if rows % 512 == 0 else LEAF
    base = start // tile
    slot = own.shape[1]
    far = mine.shape[1]
    anywhere = pl.BlockSpec(memory_space=pl.ANY)
    operands = [place, own, beside, mine, other, *weight, front]
    specs = [
        pl.BlockSpec((tile, slot), lambda i, place: (base + i, 0)),
        pl.BlockSpec((tile, slot), lambda i, place: (base + i, 0)),
        pl.BlockSpec((tile, far), lambda i, place: (i, 0)),
        pl.BlockSpec((tile, far), lambda i, place: (i, 0)),
        anywhere,
        anywhere,
        pl.BlockSpec((tile, width), lambda i, place: (base + i, 0)),
    ]
    aliases = {}
    if schur is not None:
        aliases = {len(operands): 0}
        operands.append(schur)
        specs.append(anywhere)
    return pl.pallas_call(
        functools.partial(update_kernel, start // LEAF),
        out_shape=[jax.ShapeDtypeStruct((height, width), F32), jax.ShapeDtypeStruct((rows, LEAF), F32)],
        grid_spec=pltpu.PrefetchScalarGridSpec(
            num_scalar_prefetch=1,
            grid=(rows // tile,),
            in_specs=specs,
            out_specs=[
                pl.BlockSpec((tile, width), lambda i, place: (base + i, 0)),
                pl.BlockSpec((tile, LEAF), lambda i, place: (i, 0)),
            ],
            scratch_shapes=[
                pltpu.VMEM((panel, width), BF16),
                pltpu.VMEM((panel, width), BF16),
                pltpu.SemaphoreType.DMA((2, width // min(width, 512))),
            ],
        ),
        input_output_aliases=aliases,
        compiler_params=pltpu.CompilerParams(vmem_limit_bytes=VMEM),
        cost_estimate=pl.CostEstimate(
            flops=6 * rows * panel * width, bytes_accessed=rows * width * 8 + panel * width * 4, transcendentals=0
        ),
        name="update",
    )(*operands)


def halve(value, axis):
    half = value.shape[0] // 2
    at = lax.axis_index(axis)
    mine = lax.dynamic_slice_in_dim(value, at * half, half, 0)
    return mine + swap(lax.dynamic_slice_in_dim(value, (1 - at) * half, half, 0), axis)


def double(value, axis):
    other = swap(value, axis)
    first = lax.axis_index(axis) == 0
    return jnp.concatenate([jnp.where(first, value, other), jnp.where(first, other, value)], axis=0)


def group_sum(gram):
    chips, z = lax.axis_size("z"), lax.axis_index("z")
    value = halve(halve(gram, "core"), "lo")
    parts = value.reshape(chips, value.shape[0] // chips, value.shape[1])
    total = lax.dynamic_index_in_dim(parts, z, 0, keepdims=False)
    for step in range(1, chips):
        part = lax.dynamic_index_in_dim(parts, (z + step) % chips, 0, keepdims=False)
        total = total + shift(part, "z", step)
    parts = jnp.stack([total] + [shift(total, "z", step) for step in range(1, chips)])
    value = jnp.take(parts, (z - jnp.arange(chips)) % chips, axis=0).reshape(value.shape)
    return double(double(value, "lo"), "core")


def spread_test(test_matrix, rows):
    row_count, chips = 2 * lax.axis_size("hi"), lax.axis_size("z")
    row, z, core = lax.axis_index("hi") * 2 + lax.axis_index("lo"), lax.axis_index("z"), lax.axis_index("core")
    piece = 2 * rows // row_count
    half = chips // 2
    received = []
    for turn in range(half):
        route = [
            (2 * at + h, 2 * (h * half + (at + turn) % half) + at // half) for at in range(chips) for h in range(2)
        ]
        start = (z + turn) % half * 2 * rows + row * piece
        part = lax.dynamic_slice_in_dim(test_matrix, start, piece, 0)
        received.append(lax.ppermute(part, ("z", "core"), route))
    stacked = jnp.stack(received)
    parts = []
    for turn in range(half):
        route = []
        for k in range(row_count):
            for at in range(chips):
                for e in range(2):
                    target = e * half + (turn + k) % half
                    route.append(((k * chips + at) * 2 + e, (target * chips + at) * 2 + k // half))
        which = (z - turn - row) % half
        parts.append(lax.ppermute(lax.dynamic_index_in_dim(stacked, which, 0, keepdims=False), ALL, route))
    parts = jnp.stack(parts)
    order = (row - jnp.arange(half)) % half
    return jnp.take(parts, order, axis=0).reshape(half * piece, -1)


def body(front_trailing, panel_columns, panel_rows, pivots, diag_inverse, test_matrix):
    hi_count, z_count = lax.axis_size("hi"), lax.axis_size("z")
    row_count, col_count = 2 * hi_count, 2 * z_count
    hi, lo, z, core = [lax.axis_index(name) for name in ALL]
    row, col = hi * 2 + lo, z * 2 + core
    height, width = front_trailing.shape
    depth, slot = panel_rows.shape[0], panel_columns.shape[1]
    panel = depth * row_count
    samples = test_matrix.shape[1]
    per = height // col_count
    ratio = col_count // row_count
    targets = col_count // ratio
    chunk = height // CHUNKS
    starts = list(range(0, height, chunk))
    leaf_count = per // LEAF
    row_leaf, col_leaf = row * (height // LEAF), col * (width // LEAF)

    levels = []
    for pair in range(0, CHUNKS, 2):
        first = [(pair, h) for h in range(1, z_count)]
        second = [(pair + 1, h) for h in range(1, z_count)]
        levels += [level for both in zip(first, second) for level in both]
    if CHUNKS == 4 and z_count == 4:
        levels = [(0, 1), (1, 1), (0, 2), (1, 2), (0, 3), (2, 1), (1, 3), (2, 2), (3, 1), (2, 3), (3, 2), (3, 3)]
    carried = {(j, 0): (panel_columns[at : at + chunk],) * 2 for j, at in enumerate(starts)}

    def send(index, *others):
        if index < len(levels):
            j, h = levels[index]
            right, left = after(carried[j, h - 1], *others)
            carried[j, h] = (hop(right, 1), hop(left, -1))

    def arrived(index):
        return carried[levels[index]] if index < len(levels) else ()

    def whole_chunk(j):
        parts = [
            jnp.where(z >= at, carried[j, at][0], carried[j, z_count - at][1]) for at in range(1, z_count)
        ]
        return jnp.concatenate(parts, axis=1)

    test = split_outside(test_matrix)
    send(0)
    send(1)
    beside = swap(panel_columns, "core")
    over_lo = swap(panel_rows, "lo")
    over_hi = [shift(panel_rows, "hi", step) for step in range(1, hi_count)]
    inner = lax.psum(high_dot(panel_rows, test_matrix), ("z", "core"))
    inner = lax.all_gather(inner, ("hi", "lo"), axis=0, tiled=False)

    token = ()
    halves = []
    at_level = 1
    for part in range(2):
        place = jnp.stack([(1 - core) if part == 0 else core, row_leaf, col_leaf])
        done = None
        for base, count in [(0, z_count // 2), (z_count // 2, z_count - z_count // 2)]:
            if part or base:
                send(at_level + 1, token, *arrived(at_level - 1))
                place = after(place, *arrived(at_level - 1))
                at_level += 1
            done = samples_part(front_trailing, test, place, per, base, count, z_count, done)
            token = done
        halves.append(done)
    sent, kept = swap(halves[0], "core"), halves[1]

    blocks, owners = [panel_rows, over_lo], [row, row ^ 1]
    for step, block in enumerate(over_hi, 1):
        far_hi = (hi - step) % hi_count
        blocks += [block, shift(over_lo[: depth // 2], "hi", step), swap(block[depth // 2 :], "lo")]
        owners += [far_hi * 2 + lo, far_hi * 2 + (1 - lo)]
    chips = [(z - at) % z_count for at in range(z_count)]
    order = [2 * chips[0] + core, 2 * chips[0] + 1 - core]
    order += [2 * chip + core for chip in chips[1:]] + [2 * chip + 1 - core for chip in chips[1:]]
    send(at_level + 1, token, *arrived(at_level - 1))
    inverse = after(diag_inverse.reshape(col_count, slot, panel), *arrived(at_level - 1))
    at_level += 1
    left = jnp.concatenate([lax.dynamic_index_in_dim(inverse, at, 0, keepdims=False) for at in order], axis=0)
    position = (jnp.stack(owners)[:, None] * depth + jnp.arange(depth, dtype=jnp.int32)[None, :]).reshape(panel)
    chosen = (pivots[:, None] == position[None, :]).astype(BF16)
    left_high, left_low = [
        jnp.dot(part, chosen, preferred_element_type=F32).astype(BF16) for part in split_outside(left)
    ]

    partial = (kept + sent).reshape(z_count, per, samples)
    right = left = None
    for step in range(1, z_count):
        right_part = lax.dynamic_index_in_dim(partial, jnp.minimum(z + z_count - step, z_count - 1), 0, keepdims=False)
        left_part = lax.dynamic_index_in_dim(partial, jnp.maximum(z - z_count + step, 0), 0, keepdims=False)
        right = hop(right_part if right is None else right_part + right, 1, step)
        left = hop(left_part if left is None else left_part + left, -1, step)
    sums = lax.dynamic_index_in_dim(partial, z, 0, keepdims=False) + right + left

    send(at_level + 1, left_high, *arrived(at_level - 1))
    left_high = after(left_high, *arrived(at_level - 1))
    at_level += 1
    weight = weights(left_high, left_low, blocks)

    half = col % ratio
    routes = [
        [(r * col_count + ratio * r + h, r * col_count + h * targets + m) for r in range(row_count) for h in range(ratio)]
        for m in range(targets)
    ]

    def to_owners(pieces):
        return sum(lax.ppermute(piece, ALL, route) for piece, route in zip(pieces, routes))

    def front_leaf(at):
        return lax.dynamic_slice(front_trailing, (half * width + at * LEAF, at * LEAF), (LEAF, LEAF))

    own_test = spread_test(after(test_matrix, left_low), per)
    own_front = to_owners(
        [
            after(jnp.concatenate([front_leaf(m * leaf_count + at) for at in range(leaf_count)], axis=0), left_low)
            for m in range(targets)
        ]
    )

    place = jnp.stack([core, row_leaf, col_leaf])
    schur, leaves, far = None, [], []
    token = weight[0]
    at_level -= 1
    for j, start in enumerate(starts):
        waited = [arrived(at_level), arrived(at_level + 1)]
        send(at_level + 2, token, *waited)
        send(at_level + 3, token, *waited)
        while (j, z_count - 1) not in carried or at_level + 4 < len(levels) and j == CHUNKS - 1:
            at_level += 2
            waited = [arrived(at_level), arrived(at_level + 1)]
            send(at_level + 2, token, *waited)
            send(at_level + 3, token, *waited)
        at_level += 2
        mine = whole_chunk(j)
        other = swap(mine, "core")
        far.append((mine, other))
        schur, leaf = update(after(place, *waited), panel_columns, beside, mine, other, weight, front_trailing, schur, start)
        token = leaf
        leaves.append(leaf)

    inner = jnp.concatenate([lax.dynamic_index_in_dim(inner, at, 0, keepdims=False) for at in owners], axis=0).reshape(panel, samples)
    middle = triple(left_high, left_low, *split_outside(inner))
    each = col_count // CHUNKS
    own_rows = [lax.dynamic_slice_in_dim(part, col * per, per, 0) for part in (panel_columns, beside)]
    for which in range(2):
        chosen_rows = 0.0
        for j in range(CHUNKS):
            rows = lax.dynamic_slice_in_dim(far[j][which], col % each * per, per, 0)
            chosen_rows = jnp.where(col // each == j, rows, chosen_rows)
        own_rows.append(chosen_rows)
    sums = sums - high_dot(jnp.concatenate(own_rows, axis=1), middle)

    def leaf_rows(start):
        return leaves[start // chunk][start % chunk : start % chunk + per]

    late = []
    for m in range(targets):
        piece = leaf_rows(m * per)
        for h in range(1, ratio):
            piece = jnp.where(half == h, leaf_rows(h * width + m * per), piece)
        late.append(piece)
    leaf_blocks = to_owners(late)
    change = (own_front - leaf_blocks).reshape(leaf_count, LEAF, LEAF)
    change = high_dot(change, own_test.reshape(leaf_count, LEAF, samples), (((2,), (1,)), ((0,), (0,))))
    off_samples = sums + change.reshape(per, samples)
    gram = high_dot(off_samples, off_samples, (((0,), (0,)), ((), ())))
    group_gram = (group_sum(gram) / (2 * height))[None]
    return (schur, off_samples, leaf_blocks, group_gram)


def solution(mesh):
    rows, cols = mesh.shape["row"], mesh.shape["col"]
    fine = Mesh(mesh.devices.reshape(rows // 2, 2, cols // 2, 2), ALL)
    row, col = ("hi", "lo"), ("z", "core")
    placed = (P(row, col), P(row, col), P(row, col), P(), P(), P(col, None))
    return jax.shard_map(
        body,
        mesh=fine,
        in_specs=placed,
        out_specs=(P(row, col), P(ALL, None), P(ALL, None), P(row, None, None)),
        check_vma=False,
    )
```

```python
import functools

import jax
import jax.numpy as jnp
from jax import lax
from jax.experimental import pallas as pl
from jax.experimental.pallas import tpu as pltpu
from jax.sharding import Mesh, PartitionSpec as P

LEAF = 128
VMEM = 56 * 1024 * 1024
F32 = jnp.float32
BF16 = jnp.bfloat16
ALL = ("hi", "lo", "z", "core")


def split(value):
    high = value.astype(BF16)
    return high, (value - high.astype(F32)).astype(BF16)


def split_outside(value):
    high = lax.reduce_precision(value, exponent_bits=8, mantissa_bits=7)
    return high.astype(BF16), (value - high).astype(BF16)


def triple(left_high, left_low, right_high, right_low):
    dot = functools.partial(jnp.dot, preferred_element_type=F32)
    return dot(left_high, right_high) + (dot(left_high, right_low) + dot(left_low, right_high))


def high_dot(left, right, dims=(((1,), (0,)), ((), ()))):
    return lax.dot_general(left, right, dims, precision=lax.Precision.HIGH, preferred_element_type=F32)


def swap(value, axis):
    return lax.ppermute(value, axis, [(0, 1), (1, 0)])


def shift(value, axis, step):
    count = lax.axis_size(axis)
    return lax.ppermute(value, axis, [(at, (at + step) % count) for at in range(count)])


def after(value, *others):
    return lax.optimization_barrier((value, others))[0]


def samples_kernel(place, front, test, out, test_high, test_low):
    step = pl.program_id(0)

    @pl.when(step == 0)
    def _():
        test_high[...], test_low[...] = split(test[...])

    rows, width = front.shape
    row_leaf = place[0] + step * (rows // LEAF) + lax.broadcasted_iota(jnp.int32, (rows, 1), 0) // LEAF
    col_leaf = place[1] + lax.broadcasted_iota(jnp.int32, (1, width), 1) // LEAF
    high, low = split(jnp.where(row_leaf == col_leaf, 0.0, front[...]))
    out[...] = triple(high, low, test_high[...], test_low[...])


def front_samples(place, front, test):
    height, width = front.shape
    samples = test.shape[1]
    rows = 512
    return pl.pallas_call(
        samples_kernel,
        out_shape=jax.ShapeDtypeStruct((height, samples), F32),
        grid_spec=pltpu.PrefetchScalarGridSpec(
            num_scalar_prefetch=1,
            grid=(height // rows,),
            in_specs=[
                pl.BlockSpec((rows, width), lambda s, place: (s, 0)),
                pl.BlockSpec((width, samples), lambda s, place: (0, 0), pipeline_mode=pl.Buffered(1)),
            ],
            out_specs=pl.BlockSpec((rows, samples), lambda s, place: (s, 0)),
            scratch_shapes=[pltpu.VMEM((width, samples), BF16)] * 2,
        ),
        compiler_params=pltpu.CompilerParams(vmem_limit_bytes=VMEM),
        cost_estimate=pl.CostEstimate(
            flops=6 * height * width * samples, bytes_accessed=height * width * 4, transcendentals=0
        ),
        name="samples",
    )(place, front, test)


def weights_kernel(parts, *refs):
    left_high, left_low, test = refs[:3]
    out_high, out_low, product_high, product_low, total = refs[3 + parts :]
    step = pl.program_id(0)
    high, low = split(jnp.concatenate([ref[...] for ref in refs[3 : 3 + parts]], axis=0))
    high, low = split(triple(left_high[...], left_low[...], high, low))
    out_high[...] = high
    out_low[...] = low
    part = triple(high, low, *split(test[...]))

    @pl.when(step == 0)
    def _():
        total[...] = part

    @pl.when(step > 0)
    def _():
        total[...] += part

    @pl.when(step == pl.num_programs(0) - 1)
    def _():
        product_high[...], product_low[...] = split(total[...])


def weights(left_high, left_low, test, blocks):
    panel = left_high.shape[0]
    width, samples = test.shape
    tile = min(width, 512)
    whole = pl.BlockSpec((panel, panel), lambda n: (0, 0), pipeline_mode=pl.Buffered(1))
    product = pl.BlockSpec((panel, samples), lambda n: (0, 0))
    return pl.pallas_call(
        functools.partial(weights_kernel, len(blocks)),
        out_shape=[jax.ShapeDtypeStruct((panel, width), BF16)] * 2 + [jax.ShapeDtypeStruct((panel, samples), BF16)] * 2,
        grid=(width // tile,),
        in_specs=[whole, whole, pl.BlockSpec((tile, samples), lambda n: (n, 0))]
        + [pl.BlockSpec((b.shape[0], tile), lambda n: (0, n)) for b in blocks],
        out_specs=[pl.BlockSpec((panel, tile), lambda n: (0, n))] * 2 + [product, product],
        scratch_shapes=[pltpu.VMEM((panel, samples), F32)],
        compiler_params=pltpu.CompilerParams(vmem_limit_bytes=VMEM),
        cost_estimate=pl.CostEstimate(
            flops=6 * panel * (panel + samples) * width, bytes_accessed=panel * width * 8, transcendentals=0
        ),
        name="weights",
    )(left_high, left_low, test, *blocks)


def terms_kernel(place, columns, partial, product_high, product_low, high, low, test, out):
    slots, rows, _ = columns.shape
    width = high.shape[1]
    left_high, left_low = split(jnp.concatenate([columns[at] for at in range(slots)], axis=1))
    out[...] = partial[...] - triple(left_high, left_low, product_high[...], product_low[...])
    leaf = place[0] - place[1] + pl.program_id(0) * (rows // LEAF)
    for at in range(rows // LEAF):

        @pl.when((leaf + at >= 0) & (leaf + at < width // LEAF))
        def _():
            piece = slice(at * LEAF, (at + 1) * LEAF)
            column = pl.multiple_of((leaf + at) * LEAF, LEAF)
            block = triple(
                left_high[piece], left_low[piece], high[:, pl.ds(column, LEAF)], low[:, pl.ds(column, LEAF)]
            )
            out[piece] += triple(*split(block), *split(test[pl.ds(column, LEAF)]))


def terms(place, columns, partial, weight, product, test):
    slots, height, slot = columns.shape
    panel, width = weight[0].shape
    samples = test.shape[1]
    tile = 512

    def whole(array):
        return pl.BlockSpec(array.shape, lambda i, place: (0, 0), pipeline_mode=pl.Buffered(1))

    return pl.pallas_call(
        terms_kernel,
        out_shape=jax.ShapeDtypeStruct(partial.shape, F32),
        grid_spec=pltpu.PrefetchScalarGridSpec(
            num_scalar_prefetch=1,
            grid=(height // tile,),
            in_specs=[
                pl.BlockSpec((slots, tile, slot), lambda i, place: (0, i, 0)),
                pl.BlockSpec((tile, samples), lambda i, place: (i, 0)),
                *map(whole, product),
                *map(whole, weight),
                whole(test),
            ],
            out_specs=pl.BlockSpec((tile, samples), lambda i, place: (i, 0)),
        ),
        compiler_params=pltpu.CompilerParams(vmem_limit_bytes=VMEM),
        cost_estimate=pl.CostEstimate(
            flops=6 * height * panel * samples, bytes_accessed=height * (panel + 2 * samples) * 4, transcendentals=0
        ),
        name="terms",
    )(place, columns, partial, *product, *weight, test)


def update_kernel(place, columns, high, low, front, out, leaves):
    slots = columns.shape[0]
    left_high, left_low = split(jnp.concatenate([columns[at] for at in range(slots)], axis=1))
    out[...] = front[...] - triple(left_high, left_low, high[...], low[...])
    rows, width = out.shape
    leaf = place[0] - place[1] + pl.program_id(0) * (rows // LEAF)
    for at in range(rows // LEAF):
        column = jnp.clip(leaf + at, 0, width // LEAF - 1) * LEAF
        piece = pl.ds(at * LEAF, LEAF)
        leaves[piece, :] = out[piece, pl.ds(pl.multiple_of(column, LEAF), LEAF)]


def update(place, columns, weight, front):
    slots, height, slot = columns.shape
    panel, width = weight[0].shape
    tile = 256
    whole = pl.BlockSpec((panel, width), lambda i, place: (0, 0), pipeline_mode=pl.Buffered(1))
    return pl.pallas_call(
        update_kernel,
        out_shape=[jax.ShapeDtypeStruct((height, width), F32), jax.ShapeDtypeStruct((height, LEAF), F32)],
        grid_spec=pltpu.PrefetchScalarGridSpec(
            num_scalar_prefetch=1,
            grid=(height // tile,),
            in_specs=[
                pl.BlockSpec((slots, tile, slot), lambda i, place: (0, i, 0)),
                whole,
                whole,
                pl.BlockSpec((tile, width), lambda i, place: (i, 0)),
            ],
            out_specs=[
                pl.BlockSpec((tile, width), lambda i, place: (i, 0)),
                pl.BlockSpec((tile, LEAF), lambda i, place: (i, 0)),
            ],
        ),
        compiler_params=pltpu.CompilerParams(vmem_limit_bytes=VMEM),
        cost_estimate=pl.CostEstimate(
            flops=6 * height * panel * width, bytes_accessed=height * width * 8 + panel * width * 4, transcendentals=0
        ),
        name="update",
    )(place, columns, *weight, front)


def halve(value, axis):
    half = value.shape[0] // 2
    at = lax.axis_index(axis)
    mine = lax.dynamic_slice_in_dim(value, at * half, half, 0)
    return mine + swap(lax.dynamic_slice_in_dim(value, (1 - at) * half, half, 0), axis)


def double(value, axis):
    other = swap(value, axis)
    first = lax.axis_index(axis) == 0
    return jnp.concatenate([jnp.where(first, value, other), jnp.where(first, other, value)], axis=0)


def group_sum(gram):
    chips, z = lax.axis_size("z"), lax.axis_index("z")
    value = halve(halve(gram, "core"), "lo")
    parts = value.reshape(chips, value.shape[0] // chips, value.shape[1])
    total = lax.dynamic_index_in_dim(parts, z, 0, keepdims=False)
    for step in range(1, chips):
        part = lax.dynamic_index_in_dim(parts, (z + step) % chips, 0, keepdims=False)
        total = total + shift(part, "z", step)
    parts = jnp.stack([total] + [shift(total, "z", step) for step in range(1, chips)])
    value = jnp.take(parts, (z - jnp.arange(chips)) % chips, axis=0).reshape(value.shape)
    return double(double(value, "lo"), "core")


def body(front_trailing, panel_columns, panel_rows, pivots, diag_inverse, test_matrix):
    hi_count, z_count = lax.axis_size("hi"), lax.axis_size("z")
    row_count, col_count = 2 * hi_count, 2 * z_count
    hi, lo, z, core = [lax.axis_index(name) for name in ALL]
    row, col = hi * 2 + lo, z * 2 + core
    height, width = front_trailing.shape
    depth = panel_rows.shape[0]
    panel = depth * row_count
    per = height // col_count
    ratio = col_count // row_count
    targets = col_count // ratio
    place = jnp.stack([row * (height // LEAF), col * (width // LEAF)])

    columns = lax.all_gather(panel_columns, ("z", "core"), axis=0, tiled=False)

    over_lo = swap(panel_rows, "lo")
    over_hi = [shift(panel_rows, "hi", step) for step in range(1, hi_count)]
    partial = front_samples(place, front_trailing, test_matrix)
    over_lo, *over_hi = after([over_lo, *over_hi], partial)
    blocks, owners = [panel_rows, over_lo], [row, row ^ 1]
    for step, block in enumerate(over_hi, 1):
        far_hi = (hi - step) % hi_count
        blocks += [block, shift(over_lo[: depth // 2], "hi", step), swap(block[depth // 2 :], "lo")]
        owners += [far_hi * 2 + lo, far_hi * 2 + (1 - lo)]

    position = (jnp.stack(owners)[:, None] * depth + jnp.arange(depth, dtype=jnp.int32)[None, :]).reshape(panel)
    chosen = (pivots[:, None] == position[None, :]).astype(BF16)
    left_high, left_low = [
        jnp.dot(part, chosen, preferred_element_type=F32).astype(BF16)
        for part in split_outside(after(diag_inverse, partial))
    ]
    high, low, *product = weights(left_high, left_low, test_matrix, blocks)

    partial = terms(place, columns, partial, (high, low), product, test_matrix)
    off_samples = lax.psum_scatter(partial, ("z", "core"), scatter_dimension=0, tiled=True)
    schur, leaves = update(after(place, partial), columns, (high, low), front_trailing)

    half = col % ratio
    leaf_blocks = 0
    for m in range(targets):
        piece = lax.dynamic_slice_in_dim(leaves, (half * targets + m) * per, per, 0)
        route = [
            (r * col_count + ratio * r + h, r * col_count + h * targets + m)
            for r in range(row_count)
            for h in range(ratio)
        ]
        leaf_blocks = leaf_blocks + lax.ppermute(piece, ALL, route)

    gram = high_dot(after(off_samples, leaf_blocks), off_samples, (((0,), (0,)), ((), ())))
    group_gram = (group_sum(gram) / (2 * height))[None]
    return (schur, off_samples, leaf_blocks, group_gram)


def solution(mesh):
    rows, cols = mesh.shape["row"], mesh.shape["col"]
    fine = Mesh(mesh.devices.reshape(rows // 2, 2, cols // 2, 2), ALL)
    row, col = ("hi", "lo"), ("z", "core")
    placed = (P(row, col), P(row, col), P(row, col), P(), P(), P(col, None))
    return jax.shard_map(
        body,
        mesh=fine,
        in_specs=placed,
        out_specs=(P(row, col), P(ALL, None), P(ALL, None), P(row, None, None)),
        check_vma=False,
    )
```

```python
import functools

import jax
import jax.numpy as jnp
from jax import lax
from jax.experimental import pallas as pl
from jax.experimental.pallas import tpu as pltpu
from jax.sharding import Mesh, PartitionSpec as P

LEAF = 128
VMEM = 56 * 1024 * 1024
F32 = jnp.float32
BF16 = jnp.bfloat16
ALL = ("hi", "lo", "z", "core")


def split(value):
    high = value.astype(BF16)
    return high, (value - high.astype(F32)).astype(BF16)


def split_outside(value):
    high = lax.reduce_precision(value, exponent_bits=8, mantissa_bits=7)
    return high.astype(BF16), (value - high).astype(BF16)


def triple(left_high, left_low, right_high, right_low):
    dot = functools.partial(jnp.dot, preferred_element_type=F32)
    return dot(left_high, right_high) + (dot(left_high, right_low) + dot(left_low, right_high))


def swap(value, axis):
    return lax.ppermute(value, axis, [(0, 1), (1, 0)])


def shift(value, axis, step):
    count = lax.axis_size(axis)
    return lax.ppermute(value, axis, [(at, (at + step) % count) for at in range(count)])


def after(value, *others):
    return lax.optimization_barrier((value, others))[0]


def samples_kernel(place, front, test, out, test_high, test_low):
    step = pl.program_id(0)

    @pl.when(step == 0)
    def _():
        test_high[...], test_low[...] = split(test[...])

    rows, width = front.shape
    row_leaf = place[0] + step * (rows // LEAF) + lax.broadcasted_iota(jnp.int32, (rows, 1), 0) // LEAF
    col_leaf = place[1] + lax.broadcasted_iota(jnp.int32, (1, width), 1) // LEAF
    high, low = split(jnp.where(row_leaf == col_leaf, 0.0, front[...]))
    out[...] = triple(high, low, test_high[...], test_low[...])


def front_samples(place, front, test):
    height, width = front.shape
    samples = test.shape[1]
    rows = 512
    return pl.pallas_call(
        samples_kernel,
        out_shape=jax.ShapeDtypeStruct((height, samples), F32),
        grid_spec=pltpu.PrefetchScalarGridSpec(
            num_scalar_prefetch=1,
            grid=(height // rows,),
            in_specs=[
                pl.BlockSpec((rows, width), lambda s, place: (s, 0)),
                pl.BlockSpec((width, samples), lambda s, place: (0, 0), pipeline_mode=pl.Buffered(1)),
            ],
            out_specs=pl.BlockSpec((rows, samples), lambda s, place: (s, 0)),
            scratch_shapes=[pltpu.VMEM((width, samples), BF16)] * 2,
        ),
        compiler_params=pltpu.CompilerParams(vmem_limit_bytes=VMEM),
        cost_estimate=pl.CostEstimate(
            flops=6 * height * width * samples, bytes_accessed=height * width * 4, transcendentals=0
        ),
        name="samples",
    )(place, front, test)


def weights_kernel(parts, *refs):
    left_high, left_low, test = refs[:3]
    out_high, out_low, product_high, product_low, total = refs[3 + parts :]
    step = pl.program_id(0)
    high, low = split(jnp.concatenate([ref[...] for ref in refs[3 : 3 + parts]], axis=0))
    high, low = split(triple(left_high[...], left_low[...], high, low))
    out_high[...] = high
    out_low[...] = low
    part = triple(high, low, *split(test[...]))

    @pl.when(step == 0)
    def _():
        total[...] = part

    @pl.when(step > 0)
    def _():
        total[...] += part

    @pl.when(step == pl.num_programs(0) - 1)
    def _():
        product_high[...], product_low[...] = split(total[...])


def weights(left_high, left_low, test, blocks):
    panel = left_high.shape[0]
    width, samples = test.shape
    tile = min(width, 512)
    whole = pl.BlockSpec((panel, panel), lambda n: (0, 0), pipeline_mode=pl.Buffered(1))
    product = pl.BlockSpec((panel, samples), lambda n: (0, 0))
    return pl.pallas_call(
        functools.partial(weights_kernel, len(blocks)),
        out_shape=[jax.ShapeDtypeStruct((panel, width), BF16)] * 2 + [jax.ShapeDtypeStruct((panel, samples), BF16)] * 2,
        grid=(width // tile,),
        in_specs=[whole, whole, pl.BlockSpec((tile, samples), lambda n: (n, 0))]
        + [pl.BlockSpec((b.shape[0], tile), lambda n: (0, n)) for b in blocks],
        out_specs=[pl.BlockSpec((panel, tile), lambda n: (0, n))] * 2 + [product, product],
        scratch_shapes=[pltpu.VMEM((panel, samples), F32)],
        compiler_params=pltpu.CompilerParams(vmem_limit_bytes=VMEM),
        cost_estimate=pl.CostEstimate(
            flops=6 * panel * (panel + samples) * width, bytes_accessed=panel * width * 8, transcendentals=0
        ),
        name="weights",
    )(left_high, left_low, test, *blocks)


def terms_kernel(base, place, columns, partial, product_high, product_low, high, low, test, out):
    slots, rows, _ = columns.shape
    left_high, left_low = split(jnp.concatenate([columns[at] for at in range(slots)], axis=1))
    out[...] = partial[...] - triple(left_high, left_low, product_high[...], product_low[...])
    tile = place[2] + base + pl.program_id(0)

    @pl.when((tile >= 0) & (tile < place[3]))
    def _():
        for at in range(rows // LEAF):
            piece = slice(at * LEAF, (at + 1) * LEAF)
            block = triple(left_high[piece], left_low[piece], high[:, piece], low[:, piece])
            out[piece] += triple(*split(block), *split(test[piece]))


def terms(place, columns, partial, weight, product, test, start, tile):
    slots, rows, slot = columns.shape
    panel, width = weight[0].shape
    samples = test.shape[1]
    base = start // tile
    last = width // tile - 1

    def diagonal(i, place):
        return jnp.clip(place[2] + base + i, 0, last)

    whole = pl.BlockSpec((panel, samples), lambda i, place: (0, 0), pipeline_mode=pl.Buffered(1))
    strip = pl.BlockSpec((panel, tile), lambda i, place: (0, diagonal(i, place)))
    return pl.pallas_call(
        functools.partial(terms_kernel, base),
        out_shape=jax.ShapeDtypeStruct(partial.shape, F32),
        grid_spec=pltpu.PrefetchScalarGridSpec(
            num_scalar_prefetch=1,
            grid=(rows // tile,),
            in_specs=[
                pl.BlockSpec((slots, tile, slot), lambda i, place: (0, i, 0)),
                pl.BlockSpec((tile, samples), lambda i, place: (base + i, 0)),
                whole,
                whole,
                strip,
                strip,
                pl.BlockSpec((tile, samples), lambda i, place: (diagonal(i, place), 0)),
            ],
            out_specs=pl.BlockSpec((tile, samples), lambda i, place: (base + i, 0)),
        ),
        input_output_aliases={2: 0},
        compiler_params=pltpu.CompilerParams(vmem_limit_bytes=VMEM),
        cost_estimate=pl.CostEstimate(
            flops=6 * rows * panel * samples, bytes_accessed=rows * (panel + 2 * samples) * 4, transcendentals=0
        ),
        name="terms",
    )(place, columns, partial, *product, *weight, test)


def update_kernel(tiles, place, first, second, high, low, front, out, leaves):
    slots = first.shape[0]
    step = pl.program_id(0)
    columns = [jnp.where(step < tiles, first[at], second[at]) for at in range(slots)]
    left_high, left_low = split(jnp.concatenate(columns, axis=1))
    out[...] = front[...] - triple(left_high, left_low, high[...], low[...])
    rows, width = out.shape
    leaf = place[0] - place[1] + step * (rows // LEAF)
    for at in range(rows // LEAF):
        column = jnp.clip(leaf + at, 0, width // LEAF - 1) * LEAF
        piece = pl.ds(at * LEAF, LEAF)
        leaves[piece, :] = out[piece, pl.ds(pl.multiple_of(column, LEAF), LEAF)]


def update(place, chunks, weight, front):
    slots, _, slot = chunks[0].shape
    height, width = front.shape
    panel = weight[0].shape[0]
    tile = 256
    tiles = chunks[0].shape[1] // tile
    whole = pl.BlockSpec((panel, width), lambda i, place: (0, 0), pipeline_mode=pl.Buffered(1))
    return pl.pallas_call(
        functools.partial(update_kernel, tiles),
        out_shape=[jax.ShapeDtypeStruct((height, width), F32), jax.ShapeDtypeStruct((height, LEAF), F32)],
        grid_spec=pltpu.PrefetchScalarGridSpec(
            num_scalar_prefetch=1,
            grid=(height // tile,),
            in_specs=[
                pl.BlockSpec((slots, tile, slot), lambda i, place: (0, jnp.minimum(i, tiles - 1), 0)),
                pl.BlockSpec((slots, tile, slot), lambda i, place: (0, jnp.maximum(i - tiles, 0), 0)),
                whole,
                whole,
                pl.BlockSpec((tile, width), lambda i, place: (i, 0)),
            ],
            out_specs=[
                pl.BlockSpec((tile, width), lambda i, place: (i, 0)),
                pl.BlockSpec((tile, LEAF), lambda i, place: (i, 0)),
            ],
        ),
        compiler_params=pltpu.CompilerParams(vmem_limit_bytes=VMEM),
        cost_estimate=pl.CostEstimate(
            flops=6 * height * panel * width, bytes_accessed=height * width * 8 + panel * width * 4, transcendentals=0
        ),
        name="update",
    )(place, *chunks, *weight, front)


def halve(value, axis):
    half = value.shape[0] // 2
    at = lax.axis_index(axis)
    mine = lax.dynamic_slice_in_dim(value, at * half, half, 0)
    return mine + swap(lax.dynamic_slice_in_dim(value, (1 - at) * half, half, 0), axis)


def double(value, axis):
    other = swap(value, axis)
    first = lax.axis_index(axis) == 0
    return jnp.concatenate([jnp.where(first, value, other), jnp.where(first, other, value)], axis=0)


def group_sum(gram):
    chips, z = lax.axis_size("z"), lax.axis_index("z")
    value = halve(halve(gram, "core"), "lo")
    parts = value.reshape(chips, value.shape[0] // chips, value.shape[1])
    total = lax.dynamic_index_in_dim(parts, z, 0, keepdims=False)
    for step in range(1, chips):
        part = lax.dynamic_index_in_dim(parts, (z + step) % chips, 0, keepdims=False)
        total = total + shift(part, "z", step)
    parts = jnp.stack([total] + [shift(total, "z", step) for step in range(1, chips)])
    value = jnp.take(parts, (z - jnp.arange(chips)) % chips, axis=0).reshape(value.shape)
    return double(double(value, "lo"), "core")


def pack_kernel(rows, out):
    high, low = split(rows[...])
    dot = functools.partial(
        lax.dot_general, dimension_numbers=(((0,), (0,)), ((), ())), preferred_element_type=F32
    )
    size = rows.shape[1]
    at = 0
    for start in range(0, size, LEAF):
        part, rest = slice(start, start + LEAF), slice(start, size)
        value = dot(high[:, part], high[:, rest]) + (dot(high[:, part], low[:, rest]) + dot(low[:, part], high[:, rest]))
        for column in range(0, size - start, LEAF):
            out[at : at + LEAF] = value[:, column : column + LEAF]
            at += LEAF


def packed_gram(rows):
    size = rows.shape[1]
    count = size // LEAF
    return pl.pallas_call(
        pack_kernel,
        out_shape=jax.ShapeDtypeStruct((count * (count + 1) // 2 * LEAF, LEAF), F32),
        compiler_params=pltpu.CompilerParams(vmem_limit_bytes=VMEM),
        name="gram",
    )(rows)


def unpack_kernel(divisor, blocks, out):
    size = out.shape[0]
    at = 0
    for i in range(0, size, LEAF):
        for j in range(i, size, LEAF):
            block = blocks[at : at + LEAF] / divisor
            out[i : i + LEAF, j : j + LEAF] = block
            if j > i:
                out[j : j + LEAF, i : i + LEAF] = block.T
            at += LEAF


def unpacked(blocks, size, divisor):
    return pl.pallas_call(
        functools.partial(unpack_kernel, float(divisor)),
        out_shape=jax.ShapeDtypeStruct((size, size), F32),
        compiler_params=pltpu.CompilerParams(vmem_limit_bytes=VMEM),
        name="unpack",
    )(blocks)


def spread_leaves(leaves, rows):
    row_count, chips = 2 * lax.axis_size("hi"), lax.axis_size("z")
    row, z, core = lax.axis_index("hi") * 2 + lax.axis_index("lo"), lax.axis_index("z"), lax.axis_index("core")
    piece = 2 * rows // row_count
    half = chips // 2
    width = half * 2 * rows
    region = lax.dynamic_slice_in_dim(leaves, core * width, width, 0).reshape(half, row_count, piece, LEAF)

    def part(step):
        return lax.dynamic_index_in_dim(region, (row + step) % row_count, 1, keepdims=False)

    share = jnp.where(row == z, part(0), 0.0)
    for step in range(1, row_count):
        route = []
        for r in range(row_count):
            for h in range(2):
                route.append(((r * chips + r) * 2 + h, ((r + step) % row_count * chips + r) * 2 + h))
        share = share + lax.ppermute(part(step), ALL, route)
    received = []
    for turn in range(half):
        route = [
            (2 * at + h, 2 * (h * half + (at + turn) % half) + at // half) for at in range(chips) for h in range(2)
        ]
        sent = lax.dynamic_index_in_dim(share, (z + turn) % half, 0, keepdims=False)
        received.append(lax.ppermute(sent, ("z", "core"), route))
    stacked = jnp.stack(received)
    parts = []
    for turn in range(half):
        route = []
        for k in range(row_count):
            for at in range(chips):
                for e in range(2):
                    target = e * half + (turn + k) % half
                    route.append(((k * chips + at) * 2 + e, (target * chips + at) * 2 + k // half))
        which = (z - turn - row) % half
        parts.append(lax.ppermute(lax.dynamic_index_in_dim(stacked, which, 0, keepdims=False), ALL, route))
    stacked = jnp.stack(parts)
    ordered = [lax.dynamic_index_in_dim(stacked, (row - at) % half, 0, keepdims=False) for at in range(half)]
    return jnp.concatenate(ordered, axis=0)


def body(front_trailing, panel_columns, panel_rows, pivots, diag_inverse, test_matrix):
    hi_count, z_count = lax.axis_size("hi"), lax.axis_size("z")
    row_count, col_count = 2 * hi_count, 2 * z_count
    hi, lo, z, core = [lax.axis_index(name) for name in ALL]
    row, col = hi * 2 + lo, z * 2 + core
    height, width = front_trailing.shape
    depth = panel_rows.shape[0]
    panel = depth * row_count
    per = height // col_count
    tile = height // 8
    cut = height - tile
    place = jnp.stack(
        [
            row * (height // LEAF),
            col * (width // LEAF),
            row * (height // tile) - col * (width // tile),
            jnp.int32(width // tile),
        ]
    )

    first = lax.all_gather(panel_columns[:cut], ("z", "core"), axis=0, tiled=False)
    over_lo = swap(panel_rows, "lo")
    over_hi = [shift(panel_rows, "hi", step) for step in range(1, hi_count)]
    partial = front_samples(place, front_trailing, test_matrix)
    second = lax.all_gather(after(panel_columns[cut:], over_lo), ("z", "core"), axis=0, tiled=False)
    over_lo, *over_hi = after([over_lo, *over_hi], partial)
    blocks, owners = [panel_rows, over_lo], [row, row ^ 1]
    for step, block in enumerate(over_hi, 1):
        far_hi = (hi - step) % hi_count
        blocks += [block, shift(over_lo[: depth // 2], "hi", step), swap(block[depth // 2 :], "lo")]
        owners += [far_hi * 2 + lo, far_hi * 2 + (1 - lo)]

    position = (jnp.stack(owners)[:, None] * depth + jnp.arange(depth, dtype=jnp.int32)[None, :]).reshape(panel)
    chosen = (pivots[:, None] == position[None, :]).astype(BF16)
    left_high, left_low = [
        jnp.dot(part, chosen, preferred_element_type=F32).astype(BF16)
        for part in split_outside(after(diag_inverse, partial))
    ]
    high, low, *product = weights(left_high, left_low, test_matrix, blocks)

    weight = (high, low)
    partial = terms(place, first, partial, weight, product, test_matrix, 0, tile)
    partial = terms(place, second, partial, weight, product, test_matrix, cut, tile)
    off_samples = lax.psum_scatter(partial, ("z", "core"), scatter_dimension=0, tiled=True)
    schur, leaves = update(after(place, partial), (first, second), weight, front_trailing)
    leaf_blocks = spread_leaves(leaves, per)
    samples = after(off_samples, leaf_blocks)
    gram = group_sum(packed_gram(samples))
    group_gram = unpacked(gram, samples.shape[1], 2 * height)[None]
    return (schur, off_samples, leaf_blocks, group_gram)


def solution(mesh):
    rows, cols = mesh.shape["row"], mesh.shape["col"]
    fine = Mesh(mesh.devices.reshape(rows // 2, 2, cols // 2, 2), ALL)
    row, col = ("hi", "lo"), ("z", "core")
    placed = (P(row, col), P(row, col), P(row, col), P(), P(), P(col, None))
    return jax.shard_map(
        body,
        mesh=fine,
        in_specs=placed,
        out_specs=(P(row, col), P(ALL, None), P(ALL, None), P(row, None, None)),
        check_vma=False,
    )
```

```python
import functools

import jax
import jax.numpy as jnp
from jax import lax
from jax.experimental import pallas as pl
from jax.experimental.pallas import tpu as pltpu
from jax.sharding import Mesh, PartitionSpec as P

LEAF = 128
VMEM = 56 * 1024 * 1024
F32 = jnp.float32
BF16 = jnp.bfloat16
ALL = ("hi", "lo", "z", "core")


def split(value):
    high = value.astype(BF16)
    return high, (value - high.astype(F32)).astype(BF16)


def split_outside(value):
    high = lax.reduce_precision(value, exponent_bits=8, mantissa_bits=7)
    return high.astype(BF16), (value - high).astype(BF16)


def triple(left_high, left_low, right_high, right_low):
    dot = functools.partial(jnp.dot, preferred_element_type=F32)
    return dot(left_high, right_high) + (dot(left_high, right_low) + dot(left_low, right_high))


def swap(value, axis):
    return lax.ppermute(value, axis, [(0, 1), (1, 0)])


def shift(value, axis, step):
    count = lax.axis_size(axis)
    return lax.ppermute(value, axis, [(at, (at + step) % count) for at in range(count)])


def after(value, *others):
    return lax.optimization_barrier((value, others))[0]


def samples_kernel(place, front, test, out, test_high, test_low):
    step = pl.program_id(0)

    @pl.when(step == 0)
    def _():
        test_high[...], test_low[...] = split(test[...])

    rows, width = front.shape
    row_leaf = place[0] + step * (rows // LEAF) + lax.broadcasted_iota(jnp.int32, (rows, 1), 0) // LEAF
    col_leaf = place[1] + lax.broadcasted_iota(jnp.int32, (1, width), 1) // LEAF
    high, low = split(jnp.where(row_leaf == col_leaf, 0.0, front[...]))
    out[...] = triple(high, low, test_high[...], test_low[...])


def front_samples(place, front, test):
    height, width = front.shape
    samples = test.shape[1]
    rows = 512
    return pl.pallas_call(
        samples_kernel,
        out_shape=jax.ShapeDtypeStruct((height, samples), F32),
        grid_spec=pltpu.PrefetchScalarGridSpec(
            num_scalar_prefetch=1,
            grid=(height // rows,),
            in_specs=[
                pl.BlockSpec((rows, width), lambda s, place: (s, 0)),
                pl.BlockSpec((width, samples), lambda s, place: (0, 0), pipeline_mode=pl.Buffered(1)),
            ],
            out_specs=pl.BlockSpec((rows, samples), lambda s, place: (s, 0)),
            scratch_shapes=[pltpu.VMEM((width, samples), BF16)] * 2,
        ),
        compiler_params=pltpu.CompilerParams(vmem_limit_bytes=VMEM),
        cost_estimate=pl.CostEstimate(
            flops=6 * height * width * samples, bytes_accessed=height * width * 4, transcendentals=0
        ),
        name="samples",
    )(place, front, test)


def weights_kernel(parts, *refs):
    left_high, left_low, test = refs[:3]
    out_high, out_low, product_high, product_low, total = refs[3 + parts :]
    step = pl.program_id(0)
    high, low = split(jnp.concatenate([ref[...] for ref in refs[3 : 3 + parts]], axis=0))
    high, low = split(triple(left_high[...], left_low[...], high, low))
    out_high[...] = high
    out_low[...] = low
    part = triple(high, low, *split(test[...]))

    @pl.when(step == 0)
    def _():
        total[...] = part

    @pl.when(step > 0)
    def _():
        total[...] += part

    @pl.when(step == pl.num_programs(0) - 1)
    def _():
        product_high[...], product_low[...] = split(total[...])


def weights(left_high, left_low, test, blocks):
    panel = left_high.shape[0]
    width, samples = test.shape
    tile = min(width, 512)
    whole = pl.BlockSpec((panel, panel), lambda n: (0, 0), pipeline_mode=pl.Buffered(1))
    product = pl.BlockSpec((panel, samples), lambda n: (0, 0))
    return pl.pallas_call(
        functools.partial(weights_kernel, len(blocks)),
        out_shape=[jax.ShapeDtypeStruct((panel, width), BF16)] * 2 + [jax.ShapeDtypeStruct((panel, samples), BF16)] * 2,
        grid=(width // tile,),
        in_specs=[whole, whole, pl.BlockSpec((tile, samples), lambda n: (n, 0))]
        + [pl.BlockSpec((b.shape[0], tile), lambda n: (0, n)) for b in blocks],
        out_specs=[pl.BlockSpec((panel, tile), lambda n: (0, n))] * 2 + [product, product],
        scratch_shapes=[pltpu.VMEM((panel, samples), F32)],
        compiler_params=pltpu.CompilerParams(vmem_limit_bytes=VMEM),
        cost_estimate=pl.CostEstimate(
            flops=6 * panel * (panel + samples) * width, bytes_accessed=panel * width * 8, transcendentals=0
        ),
        name="weights",
    )(left_high, left_low, test, *blocks)


def terms_kernel(base, place, columns, partial, product_high, product_low, high, low, test, *refs):
    out, blocks = refs[-2:]
    slots, rows, _ = columns.shape
    left_high, left_low = split(jnp.concatenate([columns[at] for at in range(slots)], axis=1))
    out[...] = partial[...] - triple(left_high, left_low, product_high[...], product_low[...])
    tile = place[2] + base + pl.program_id(0)

    @pl.when((tile >= 0) & (tile < place[3]))
    def _():
        for at in range(rows // LEAF):
            piece = slice(at * LEAF, (at + 1) * LEAF)
            block = triple(left_high[piece], left_low[piece], high[:, piece], low[:, piece])
            out[piece] += triple(*split(block), *split(test[piece]))
            blocks[piece] = block


def terms(place, columns, partial, blocks, weight, product, test, start, tile):
    slots, rows, slot = columns.shape
    panel, width = weight[0].shape
    samples = test.shape[1]
    base = start // tile
    last = width // tile - 1

    def diagonal(i, place):
        return jnp.clip(place[2] + base + i, 0, last)

    whole = pl.BlockSpec((panel, samples), lambda i, place: (0, 0), pipeline_mode=pl.Buffered(1))
    strip = pl.BlockSpec((panel, tile), lambda i, place: (0, diagonal(i, place)))
    operands = [place, columns, partial, *product, *weight, test]
    specs = [
        pl.BlockSpec((slots, tile, slot), lambda i, place: (0, i, 0)),
        pl.BlockSpec((tile, samples), lambda i, place: (base + i, 0)),
        whole,
        whole,
        strip,
        strip,
        pl.BlockSpec((tile, samples), lambda i, place: (diagonal(i, place), 0)),
    ]
    aliases = {2: 0}
    if blocks is not None:
        aliases[len(operands)] = 1
        operands.append(blocks)
        specs.append(pl.BlockSpec(memory_space=pl.ANY))
    return pl.pallas_call(
        functools.partial(terms_kernel, base),
        out_shape=[
            jax.ShapeDtypeStruct(partial.shape, F32),
            jax.ShapeDtypeStruct((partial.shape[0], LEAF), F32),
        ],
        grid_spec=pltpu.PrefetchScalarGridSpec(
            num_scalar_prefetch=1,
            grid=(rows // tile,),
            in_specs=specs,
            out_specs=[
                pl.BlockSpec((tile, samples), lambda i, place: (base + i, 0)),
                pl.BlockSpec((tile, LEAF), lambda i, place: (base + i, 0)),
            ],
        ),
        input_output_aliases=aliases,
        compiler_params=pltpu.CompilerParams(vmem_limit_bytes=VMEM),
        cost_estimate=pl.CostEstimate(
            flops=6 * rows * panel * samples, bytes_accessed=rows * (panel + 2 * samples) * 4, transcendentals=0
        ),
        name="terms",
    )(*operands)


def leaves_kernel(place, front, blocks, out):
    for at in range(0, out.shape[0], LEAF):
        piece = slice(at, at + LEAF)
        out[piece] = front[piece, piece] - blocks[piece]


def leaf_blocks_here(place, front, blocks, tile):
    width = front.shape[1]
    return pl.pallas_call(
        leaves_kernel,
        out_shape=jax.ShapeDtypeStruct((width, LEAF), F32),
        grid_spec=pltpu.PrefetchScalarGridSpec(
            num_scalar_prefetch=1,
            grid=(width // tile,),
            in_specs=[
                pl.BlockSpec((tile, tile), lambda i, place: (place[4] + i, i)),
                pl.BlockSpec((tile, LEAF), lambda i, place: (place[4] + i, 0)),
            ],
            out_specs=pl.BlockSpec((tile, LEAF), lambda i, place: (i, 0)),
        ),
        compiler_params=pltpu.CompilerParams(vmem_limit_bytes=VMEM),
        cost_estimate=pl.CostEstimate(flops=width * LEAF, bytes_accessed=width * tile * 4, transcendentals=0),
        name="leaves",
    )(place, front, blocks)


def update_kernel(tiles, first, second, high, low, front, out):
    slots = first.shape[0]
    step = pl.program_id(0)
    columns = [jnp.where(step < tiles, first[at], second[at]) for at in range(slots)]
    left_high, left_low = split(jnp.concatenate(columns, axis=1))
    out[...] = front[...] - triple(left_high, left_low, high[...], low[...])


def update(chunks, weight, front):
    slots, _, slot = chunks[0].shape
    height, width = front.shape
    panel = weight[0].shape[0]
    tile = 256
    tiles = chunks[0].shape[1] // tile
    whole = pl.BlockSpec((panel, width), lambda i: (0, 0), pipeline_mode=pl.Buffered(1))
    return pl.pallas_call(
        functools.partial(update_kernel, tiles),
        out_shape=jax.ShapeDtypeStruct((height, width), F32),
        grid=(height // tile,),
        in_specs=[
            pl.BlockSpec((slots, tile, slot), lambda i: (0, jnp.minimum(i, tiles - 1), 0)),
            pl.BlockSpec((slots, tile, slot), lambda i: (0, jnp.maximum(i - tiles, 0), 0)),
            whole,
            whole,
            pl.BlockSpec((tile, width), lambda i: (i, 0)),
        ],
        out_specs=pl.BlockSpec((tile, width), lambda i: (i, 0)),
        compiler_params=pltpu.CompilerParams(vmem_limit_bytes=VMEM),
        cost_estimate=pl.CostEstimate(
            flops=6 * height * panel * width, bytes_accessed=height * width * 8 + panel * width * 4, transcendentals=0
        ),
        name="update",
    )(*chunks, *weight, front)


def halve(value, axis):
    half = value.shape[0] // 2
    at = lax.axis_index(axis)
    mine = lax.dynamic_slice_in_dim(value, at * half, half, 0)
    return mine + swap(lax.dynamic_slice_in_dim(value, (1 - at) * half, half, 0), axis)


def double(value, axis):
    other = swap(value, axis)
    first = lax.axis_index(axis) == 0
    return jnp.concatenate([jnp.where(first, value, other), jnp.where(first, other, value)], axis=0)


def group_sum(gram):
    chips, z = lax.axis_size("z"), lax.axis_index("z")
    value = halve(gram, "core")
    parts = value.reshape(chips, value.shape[0] // chips, value.shape[1])
    total = lax.dynamic_index_in_dim(parts, z, 0, keepdims=False)
    for step in range(1, chips):
        part = lax.dynamic_index_in_dim(parts, (z + step) % chips, 0, keepdims=False)
        total = total + shift(part, "z", step)
    total = total + swap(total, "lo")
    parts = jnp.stack([total] + [shift(total, "z", step) for step in range(1, chips)])
    value = jnp.take(parts, (z - jnp.arange(chips)) % chips, axis=0).reshape(value.shape)
    return double(value, "core")


def pack_kernel(rows, out):
    high, low = split(rows[...])
    dot = functools.partial(
        lax.dot_general, dimension_numbers=(((0,), (0,)), ((), ())), preferred_element_type=F32
    )
    size = rows.shape[1]
    at = 0
    for start in range(0, size, LEAF):
        part, rest = slice(start, start + LEAF), slice(start, size)
        value = dot(high[:, part], high[:, rest]) + (dot(high[:, part], low[:, rest]) + dot(low[:, part], high[:, rest]))
        for column in range(0, size - start, LEAF):
            out[at : at + LEAF] = value[:, column : column + LEAF]
            at += LEAF


def packed_gram(rows):
    size = rows.shape[1]
    count = size // LEAF
    return pl.pallas_call(
        pack_kernel,
        out_shape=jax.ShapeDtypeStruct((count * (count + 1) // 2 * LEAF, LEAF), F32),
        compiler_params=pltpu.CompilerParams(vmem_limit_bytes=VMEM),
        name="gram",
    )(rows)


def unpack_kernel(divisor, blocks, out):
    size = out.shape[0]
    at = 0
    for i in range(0, size, LEAF):
        for j in range(i, size, LEAF):
            block = blocks[at : at + LEAF] / divisor
            out[i : i + LEAF, j : j + LEAF] = block
            if j > i:
                out[j : j + LEAF, i : i + LEAF] = block.T
            at += LEAF


def unpacked(blocks, size, divisor):
    return pl.pallas_call(
        functools.partial(unpack_kernel, float(divisor)),
        out_shape=jax.ShapeDtypeStruct((size, size), F32),
        compiler_params=pltpu.CompilerParams(vmem_limit_bytes=VMEM),
        name="unpack",
    )(blocks)


def spread_leaves(region, schur, rows):
    row_count, chips = 2 * lax.axis_size("hi"), lax.axis_size("z")
    row, z = lax.axis_index("hi") * 2 + lax.axis_index("lo"), lax.axis_index("z")
    piece = 2 * rows // row_count
    half = chips // 2
    region = region.reshape(half, row_count, piece, LEAF)

    def part(step):
        return lax.dynamic_index_in_dim(region, (row + step) % row_count, 1, keepdims=False)

    share = jnp.where(row == z, part(0), 0.0)
    for step in range(1, row_count):
        route = []
        for r in range(row_count):
            for h in range(2):
                route.append(((r * chips + r) * 2 + h, ((r + step) % row_count * chips + r) * 2 + h))
        share = share + lax.ppermute(part(step), ALL, route)
    share = after(share, schur)
    received = []
    for turn in range(half):
        route = [
            (2 * at + h, 2 * (h * half + (at + turn) % half) + at // half) for at in range(chips) for h in range(2)
        ]
        sent = lax.dynamic_index_in_dim(share, (z + turn) % half, 0, keepdims=False)
        received.append(lax.ppermute(sent, ("z", "core"), route))
    stacked = jnp.stack(received)
    parts = []
    for turn in range(half):
        route = []
        for k in range(row_count):
            for at in range(chips):
                for e in range(2):
                    target = e * half + (turn + k) % half
                    route.append(((k * chips + at) * 2 + e, (target * chips + at) * 2 + k // half))
        which = (z - turn - row) % half
        parts.append(lax.ppermute(lax.dynamic_index_in_dim(stacked, which, 0, keepdims=False), ALL, route))
    stacked = jnp.stack(parts)
    ordered = [lax.dynamic_index_in_dim(stacked, (row - at) % half, 0, keepdims=False) for at in range(half)]
    return jnp.concatenate(ordered, axis=0)


def body(front_trailing, panel_columns, panel_rows, pivots, diag_inverse, test_matrix):
    hi_count, z_count = lax.axis_size("hi"), lax.axis_size("z")
    row_count, col_count = 2 * hi_count, 2 * z_count
    hi, lo, z, core = [lax.axis_index(name) for name in ALL]
    row, col = hi * 2 + lo, z * 2 + core
    height, width = front_trailing.shape
    depth = panel_rows.shape[0]
    panel = depth * row_count
    per = height // col_count
    tile = height // 8
    cut = height - tile
    place = jnp.stack(
        [
            row * (height // LEAF),
            col * (width // LEAF),
            row * (height // tile) - col * (width // tile),
            jnp.int32(width // tile),
            col % (col_count // row_count) * (width // tile),
        ]
    )

    first = lax.all_gather(panel_columns[:cut], ("z", "core"), axis=0, tiled=False)
    over_lo = swap(panel_rows, "lo")
    over_hi = [shift(panel_rows, "hi", step) for step in range(1, hi_count)]
    partial = front_samples(place, front_trailing, test_matrix)
    second = lax.all_gather(after(panel_columns[cut:], over_lo), ("z", "core"), axis=0, tiled=False)
    over_lo, *over_hi = after([over_lo, *over_hi], partial)
    blocks, owners = [panel_rows, over_lo], [row, row ^ 1]
    for step, block in enumerate(over_hi, 1):
        far_hi = (hi - step) % hi_count
        blocks += [block, shift(over_lo[: depth // 2], "hi", step), swap(block[depth // 2 :], "lo")]
        owners += [far_hi * 2 + lo, far_hi * 2 + (1 - lo)]

    position = (jnp.stack(owners)[:, None] * depth + jnp.arange(depth, dtype=jnp.int32)[None, :]).reshape(panel)
    chosen = (pivots[:, None] == position[None, :]).astype(BF16)
    left_high, left_low = [
        jnp.dot(part, chosen, preferred_element_type=F32).astype(BF16)
        for part in split_outside(after(diag_inverse, partial))
    ]
    high, low, *product = weights(left_high, left_low, test_matrix, blocks)

    weight = (high, low)
    partial, blocks = terms(place, first, partial, None, weight, product, test_matrix, 0, tile)
    partial, blocks = terms(place, second, partial, blocks, weight, product, test_matrix, cut, tile)
    off_samples = lax.psum_scatter(partial, ("z", "core"), scatter_dimension=0, tiled=True)

    leaves = leaf_blocks_here(place, front_trailing, blocks, tile)
    schur = update((first, second), (after(high, partial), low), front_trailing)
    leaf_blocks = spread_leaves(leaves, schur, per)
    samples = after(off_samples, leaf_blocks)
    gram = group_sum(packed_gram(samples))
    group_gram = unpacked(gram, samples.shape[1], 2 * height)[None]
    return (schur, off_samples, leaf_blocks, group_gram)


def solution(mesh):
    rows, cols = mesh.shape["row"], mesh.shape["col"]
    fine = Mesh(mesh.devices.reshape(rows // 2, 2, cols // 2, 2), ALL)
    row, col = ("hi", "lo"), ("z", "core")
    placed = (P(row, col), P(row, col), P(row, col), P(), P(), P(col, None))
    return jax.shard_map(
        body,
        mesh=fine,
        in_specs=placed,
        out_specs=(P(row, col), P(ALL, None), P(ALL, None), P(row, None, None)),
        check_vma=False,
    )
```

```python
import functools

import jax
import jax.numpy as jnp
from jax import lax
from jax.experimental import pallas as pl
from jax.experimental.pallas import tpu as pltpu
from jax.sharding import Mesh, PartitionSpec as P

LEAF = 128
VMEM = 56 * 1024 * 1024
F32 = jnp.float32
BF16 = jnp.bfloat16
ALL = ("hi", "lo", "z", "core")


def split(value):
    high = value.astype(BF16)
    return high, (value - high.astype(F32)).astype(BF16)


def split_outside(value):
    high = lax.reduce_precision(value, exponent_bits=8, mantissa_bits=7)
    return high.astype(BF16), (value - high).astype(BF16)


def triple(left_high, left_low, right_high, right_low):
    dot = functools.partial(jnp.dot, preferred_element_type=F32)
    return dot(left_high, right_high) + (dot(left_high, right_low) + dot(left_low, right_high))


def swap(value, axis):
    return lax.ppermute(value, axis, [(0, 1), (1, 0)])


def shift(value, axis, step):
    count = lax.axis_size(axis)
    return lax.ppermute(value, axis, [(at, (at + step) % count) for at in range(count)])


def after(value, *others):
    return lax.optimization_barrier((value, others))[0]


def samples_kernel(place, front, test, out, test_high, test_low):
    step = pl.program_id(0)

    @pl.when(step == 0)
    def _():
        test_high[...], test_low[...] = split(test[...])

    rows, width = front.shape
    row_leaf = place[0] + step * (rows // LEAF) + lax.broadcasted_iota(jnp.int32, (rows, 1), 0) // LEAF
    col_leaf = place[1] + lax.broadcasted_iota(jnp.int32, (1, width), 1) // LEAF
    high, low = split(jnp.where(row_leaf == col_leaf, 0.0, front[...]))
    out[...] = triple(high, low, test_high[...], test_low[...])


def front_samples(place, front, test):
    height, width = front.shape
    samples = test.shape[1]
    rows = 512
    return pl.pallas_call(
        samples_kernel,
        out_shape=jax.ShapeDtypeStruct((height, samples), F32),
        grid_spec=pltpu.PrefetchScalarGridSpec(
            num_scalar_prefetch=1,
            grid=(height // rows,),
            in_specs=[
                pl.BlockSpec((rows, width), lambda s, place: (s, 0)),
                pl.BlockSpec((width, samples), lambda s, place: (0, 0), pipeline_mode=pl.Buffered(1)),
            ],
            out_specs=pl.BlockSpec((rows, samples), lambda s, place: (s, 0)),
            scratch_shapes=[pltpu.VMEM((width, samples), BF16)] * 2,
        ),
        compiler_params=pltpu.CompilerParams(vmem_limit_bytes=VMEM),
        cost_estimate=pl.CostEstimate(
            flops=6 * height * width * samples, bytes_accessed=height * width * 4, transcendentals=0
        ),
        name="samples",
    )(place, front, test)


def weights_kernel(parts, *refs):
    left_high, left_low, test = refs[:3]
    out_high, out_low, product_high, product_low, total = refs[3 + parts :]
    step = pl.program_id(0)
    high, low = split(jnp.concatenate([ref[...] for ref in refs[3 : 3 + parts]], axis=0))
    high, low = split(triple(left_high[...], left_low[...], high, low))
    out_high[...] = high
    out_low[...] = low
    part = triple(high, low, *split(test[...]))

    @pl.when(step == 0)
    def _():
        total[...] = part

    @pl.when(step > 0)
    def _():
        total[...] += part

    @pl.when(step == pl.num_programs(0) - 1)
    def _():
        product_high[...], product_low[...] = split(total[...])


def weights(left_high, left_low, test, blocks):
    panel = left_high.shape[0]
    width, samples = test.shape
    tile = min(width, 512)
    whole = pl.BlockSpec((panel, panel), lambda n: (0, 0), pipeline_mode=pl.Buffered(1))
    product = pl.BlockSpec((panel, samples), lambda n: (0, 0))
    return pl.pallas_call(
        functools.partial(weights_kernel, len(blocks)),
        out_shape=[jax.ShapeDtypeStruct((panel, width), BF16)] * 2 + [jax.ShapeDtypeStruct((panel, samples), BF16)] * 2,
        grid=(width // tile,),
        in_specs=[whole, whole, pl.BlockSpec((tile, samples), lambda n: (n, 0))]
        + [pl.BlockSpec((b.shape[0], tile), lambda n: (0, n)) for b in blocks],
        out_specs=[pl.BlockSpec((panel, tile), lambda n: (0, n))] * 2 + [product, product],
        scratch_shapes=[pltpu.VMEM((panel, samples), F32)],
        compiler_params=pltpu.CompilerParams(vmem_limit_bytes=VMEM),
        cost_estimate=pl.CostEstimate(
            flops=6 * panel * (panel + samples) * width, bytes_accessed=panel * width * 8, transcendentals=0
        ),
        name="weights",
    )(left_high, left_low, test, *blocks)


def terms_kernel(base, place, columns, partial, product_high, product_low, high, low, test, *refs):
    out, blocks = refs[-2:]
    slots, rows, _ = columns.shape
    left_high, left_low = split(jnp.concatenate([columns[at] for at in range(slots)], axis=1))
    out[...] = partial[...] - triple(left_high, left_low, product_high[...], product_low[...])
    tile = place[2] + base + pl.program_id(0)

    @pl.when((tile >= 0) & (tile < place[3]))
    def _():
        for at in range(rows // LEAF):
            piece = slice(at * LEAF, (at + 1) * LEAF)
            block = triple(left_high[piece], left_low[piece], high[:, piece], low[:, piece])
            out[piece] += triple(*split(block), *split(test[piece]))
            blocks[piece] = block


def terms(place, columns, partial, blocks, weight, product, test, start, tile):
    slots, rows, slot = columns.shape
    panel, width = weight[0].shape
    samples = test.shape[1]
    base = start // tile
    last = width // tile - 1

    def diagonal(i, place):
        return jnp.clip(place[2] + base + i, 0, last)

    whole = pl.BlockSpec((panel, samples), lambda i, place: (0, 0), pipeline_mode=pl.Buffered(1))
    strip = pl.BlockSpec((panel, tile), lambda i, place: (0, diagonal(i, place)))
    operands = [place, columns, partial, *product, *weight, test]
    specs = [
        pl.BlockSpec((slots, tile, slot), lambda i, place: (0, i, 0)),
        pl.BlockSpec((tile, samples), lambda i, place: (base + i, 0)),
        whole,
        whole,
        strip,
        strip,
        pl.BlockSpec((tile, samples), lambda i, place: (diagonal(i, place), 0)),
    ]
    aliases = {2: 0}
    if blocks is not None:
        aliases[len(operands)] = 1
        operands.append(blocks)
        specs.append(pl.BlockSpec(memory_space=pl.ANY))
    return pl.pallas_call(
        functools.partial(terms_kernel, base),
        out_shape=[
            jax.ShapeDtypeStruct(partial.shape, F32),
            jax.ShapeDtypeStruct((partial.shape[0], LEAF), F32),
        ],
        grid_spec=pltpu.PrefetchScalarGridSpec(
            num_scalar_prefetch=1,
            grid=(rows // tile,),
            in_specs=specs,
            out_specs=[
                pl.BlockSpec((tile, samples), lambda i, place: (base + i, 0)),
                pl.BlockSpec((tile, LEAF), lambda i, place: (base + i, 0)),
            ],
        ),
        input_output_aliases=aliases,
        compiler_params=pltpu.CompilerParams(vmem_limit_bytes=VMEM),
        cost_estimate=pl.CostEstimate(
            flops=6 * rows * panel * samples, bytes_accessed=rows * (panel + 2 * samples) * 4, transcendentals=0
        ),
        name="terms",
    )(*operands)


def leaves_kernel(place, front, blocks, out):
    for at in range(0, out.shape[0], LEAF):
        piece = slice(at, at + LEAF)
        out[piece] = front[piece, piece] - blocks[piece]


def leaf_blocks_here(place, front, blocks, tile):
    width = front.shape[1]
    return pl.pallas_call(
        leaves_kernel,
        out_shape=jax.ShapeDtypeStruct((width, LEAF), F32),
        grid_spec=pltpu.PrefetchScalarGridSpec(
            num_scalar_prefetch=1,
            grid=(width // tile,),
            in_specs=[
                pl.BlockSpec((tile, tile), lambda i, place: (place[4] + i, i)),
                pl.BlockSpec((tile, LEAF), lambda i, place: (place[4] + i, 0)),
            ],
            out_specs=pl.BlockSpec((tile, LEAF), lambda i, place: (i, 0)),
        ),
        compiler_params=pltpu.CompilerParams(vmem_limit_bytes=VMEM),
        cost_estimate=pl.CostEstimate(flops=width * LEAF, bytes_accessed=width * tile * 4, transcendentals=0),
        name="leaves",
    )(place, front, blocks)


def update_kernel(tiles, first, second, high, low, front, out):
    slots = first.shape[0]
    step = pl.program_id(0)
    columns = [jnp.where(step < tiles, first[at], second[at]) for at in range(slots)]
    left_high, left_low = split(jnp.concatenate(columns, axis=1))
    out[...] = front[...] - triple(left_high, left_low, high[...], low[...])


def update(chunks, weight, front):
    slots, _, slot = chunks[0].shape
    height, width = front.shape
    panel = weight[0].shape[0]
    tile = 256
    tiles = chunks[0].shape[1] // tile
    whole = pl.BlockSpec((panel, width), lambda i: (0, 0), pipeline_mode=pl.Buffered(1))
    return pl.pallas_call(
        functools.partial(update_kernel, tiles),
        out_shape=jax.ShapeDtypeStruct((height, width), F32),
        grid=(height // tile,),
        in_specs=[
            pl.BlockSpec((slots, tile, slot), lambda i: (0, jnp.minimum(i, tiles - 1), 0)),
            pl.BlockSpec((slots, tile, slot), lambda i: (0, jnp.maximum(i - tiles, 0), 0)),
            whole,
            whole,
            pl.BlockSpec((tile, width), lambda i: (i, 0)),
        ],
        out_specs=pl.BlockSpec((tile, width), lambda i: (i, 0)),
        compiler_params=pltpu.CompilerParams(vmem_limit_bytes=VMEM),
        cost_estimate=pl.CostEstimate(
            flops=6 * height * panel * width, bytes_accessed=height * width * 8 + panel * width * 4, transcendentals=0
        ),
        name="update",
    )(*chunks, *weight, front)


def chips_sum(value):
    chips, z = lax.axis_size("z"), lax.axis_index("z")
    parts = value.reshape(chips, value.shape[0] // chips, value.shape[1])
    total = lax.dynamic_index_in_dim(parts, z, 0, keepdims=False)
    for step in range(1, chips):
        part = lax.dynamic_index_in_dim(parts, (z + step) % chips, 0, keepdims=False)
        total = total + shift(part, "z", step)
    total = total + swap(total, "lo")
    parts = jnp.stack([total] + [shift(total, "z", step) for step in range(1, chips)])
    return jnp.take(parts, (z - jnp.arange(chips)) % chips, axis=0).reshape(value.shape)


def pack_kernel(core, rows, mine, other, blocks):
    high, low = split(rows[...])
    dot = functools.partial(
        lax.dot_general, dimension_numbers=(((0,), (0,)), ((), ())), preferred_element_type=F32
    )
    size = rows.shape[1]
    at = 0
    for start in range(0, size, LEAF):
        part, rest = slice(start, start + LEAF), slice(start, size)
        value = dot(high[:, part], high[:, rest]) + (dot(high[:, part], low[:, rest]) + dot(low[:, part], high[:, rest]))
        for column in range(0, size - start, LEAF):
            blocks[at : at + LEAF] = value[:, column : column + LEAF]
            at += LEAF
    half = at // 2
    first = core[0] == 0
    mine[...] = jnp.where(first, blocks[:half], blocks[half:])
    other[...] = jnp.where(first, blocks[half:], blocks[:half])


def packed_gram(core, rows):
    size = rows.shape[1]
    count = size // LEAF
    total = count * (count + 1) // 2 * LEAF
    return pl.pallas_call(
        pack_kernel,
        out_shape=[jax.ShapeDtypeStruct((total // 2, LEAF), F32)] * 2,
        in_specs=[pl.BlockSpec(memory_space=pltpu.SMEM), pl.BlockSpec(memory_space=pltpu.VMEM)],
        out_specs=[pl.BlockSpec(memory_space=pltpu.VMEM)] * 2,
        scratch_shapes=[pltpu.VMEM((total, LEAF), F32)],
        compiler_params=pltpu.CompilerParams(vmem_limit_bytes=VMEM),
        name="gram",
    )(core, rows)


def unpack_kernel(divisor, core, mine, other, out):
    size, half = out.shape[0], mine.shape[0]
    first = core[0] == 0
    at = 0
    for i in range(0, size, LEAF):
        for j in range(i, size, LEAF):
            low = at < half
            piece = slice(at % half, at % half + LEAF)
            block = jnp.where(first == low, mine[piece], other[piece]) / divisor
            out[i : i + LEAF, j : j + LEAF] = block
            if j > i:
                out[j : j + LEAF, i : i + LEAF] = block.T
            at += LEAF


def unpacked(core, mine, other, size, divisor):
    return pl.pallas_call(
        functools.partial(unpack_kernel, float(divisor)),
        out_shape=jax.ShapeDtypeStruct((size, size), F32),
        in_specs=[pl.BlockSpec(memory_space=pltpu.SMEM)] + [pl.BlockSpec(memory_space=pltpu.VMEM)] * 2,
        out_specs=pl.BlockSpec(memory_space=pltpu.VMEM),
        compiler_params=pltpu.CompilerParams(vmem_limit_bytes=VMEM),
        name="unpack",
    )(core, mine, other)


def leaves_to_rows(region, rows):
    row_count, chips = 2 * lax.axis_size("hi"), lax.axis_size("z")
    row, z = lax.axis_index("hi") * 2 + lax.axis_index("lo"), lax.axis_index("z")
    piece = 2 * rows // row_count
    half = chips // 2
    region = region.reshape(half, row_count, piece, LEAF)

    def part(step):
        return lax.dynamic_index_in_dim(region, (row + step) % row_count, 1, keepdims=False)

    share = jnp.where(row == z, part(0), 0.0)
    for step in range(1, row_count):
        route = []
        for r in range(row_count):
            for h in range(2):
                route.append(((r * chips + r) * 2 + h, ((r + step) % row_count * chips + r) * 2 + h))
        share = share + lax.ppermute(part(step), ALL, route)
    return share


def leaves_along(share):
    chips, z = lax.axis_size("z"), lax.axis_index("z")
    half = chips // 2
    received = []
    for turn in range(half):
        route = [
            (2 * at + h, 2 * (h * half + (at + turn) % half) + at // half) for at in range(chips) for h in range(2)
        ]
        sent = lax.dynamic_index_in_dim(share, (z + turn) % half, 0, keepdims=False)
        received.append(lax.ppermute(sent, ("z", "core"), route))
    return received


def leaves_across(received):
    row_count, chips = 2 * lax.axis_size("hi"), lax.axis_size("z")
    row, z = lax.axis_index("hi") * 2 + lax.axis_index("lo"), lax.axis_index("z")
    half = chips // 2
    stacked = jnp.stack(received)
    parts = []
    for turn in range(half):
        route = []
        for k in range(row_count):
            for at in range(chips):
                for e in range(2):
                    target = e * half + (turn + k) % half
                    route.append(((k * chips + at) * 2 + e, (target * chips + at) * 2 + k // half))
        which = (z - turn - row) % half
        parts.append(lax.ppermute(lax.dynamic_index_in_dim(stacked, which, 0, keepdims=False), ALL, route))
    stacked = jnp.stack(parts)
    ordered = [lax.dynamic_index_in_dim(stacked, (row - at) % half, 0, keepdims=False) for at in range(half)]
    return jnp.concatenate(ordered, axis=0)


def body(front_trailing, panel_columns, panel_rows, pivots, diag_inverse, test_matrix):
    hi_count, z_count = lax.axis_size("hi"), lax.axis_size("z")
    row_count, col_count = 2 * hi_count, 2 * z_count
    hi, lo, z, core = [lax.axis_index(name) for name in ALL]
    row, col = hi * 2 + lo, z * 2 + core
    height, width = front_trailing.shape
    depth = panel_rows.shape[0]
    panel = depth * row_count
    per = height // col_count
    tile = height // 8
    cut = height - tile
    place = jnp.stack(
        [
            row * (height // LEAF),
            col * (width // LEAF),
            row * (height // tile) - col * (width // tile),
            jnp.int32(width // tile),
            col % (col_count // row_count) * (width // tile),
        ]
    )

    first = lax.all_gather(panel_columns[:cut], ("z", "core"), axis=0, tiled=False)
    over_lo = swap(panel_rows, "lo")
    over_hi = [shift(panel_rows, "hi", step) for step in range(1, hi_count)]
    partial = front_samples(place, front_trailing, test_matrix)
    second = lax.all_gather(after(panel_columns[cut:], over_lo), ("z", "core"), axis=0, tiled=False)
    over_lo, *over_hi = after([over_lo, *over_hi], partial)
    blocks, owners = [panel_rows, over_lo], [row, row ^ 1]
    for step, block in enumerate(over_hi, 1):
        far_hi = (hi - step) % hi_count
        blocks += [block, shift(over_lo[: depth // 2], "hi", step), swap(block[depth // 2 :], "lo")]
        owners += [far_hi * 2 + lo, far_hi * 2 + (1 - lo)]

    position = (jnp.stack(owners)[:, None] * depth + jnp.arange(depth, dtype=jnp.int32)[None, :]).reshape(panel)
    chosen = (pivots[:, None] == position[None, :]).astype(BF16)
    left_high, left_low = [
        jnp.dot(part, chosen, preferred_element_type=F32).astype(BF16)
        for part in split_outside(after(diag_inverse, partial))
    ]
    high, low, *product = weights(left_high, left_low, test_matrix, blocks)

    weight = (high, low)
    partial, blocks = terms(place, first, partial, None, weight, product, test_matrix, 0, tile)
    partial, blocks = terms(place, second, partial, blocks, weight, product, test_matrix, cut, tile)
    off_samples = lax.psum_scatter(partial, ("z", "core"), scatter_dimension=0, tiled=True)

    leaves = leaf_blocks_here(place, front_trailing, blocks, tile)
    share = leaves_to_rows(leaves, per)
    received = leaves_along(share)
    schur = update((first, second), (after(high, partial, share), low), front_trailing)
    received = after(received, schur)
    leaf_blocks = leaves_across(received)
    cores = core.reshape(1)
    mine, other = packed_gram(cores, after(off_samples, leaf_blocks))
    mine = chips_sum(mine + swap(other, "core"))
    group_gram = unpacked(cores, mine, swap(mine, "core"), off_samples.shape[1], 2 * height)[None]
    return (schur, off_samples, leaf_blocks, group_gram)


def solution(mesh):
    rows, cols = mesh.shape["row"], mesh.shape["col"]
    fine = Mesh(mesh.devices.reshape(rows // 2, 2, cols // 2, 2), ALL)
    row, col = ("hi", "lo"), ("z", "core")
    placed = (P(row, col), P(row, col), P(row, col), P(), P(), P(col, None))
    return jax.shard_map(
        body,
        mesh=fine,
        in_specs=placed,
        out_specs=(P(row, col), P(ALL, None), P(ALL, None), P(row, None, None)),
        check_vma=False,
    )
```

```python
import functools

import jax
import jax.numpy as jnp
from jax import lax
from jax.experimental import pallas as pl
from jax.experimental.pallas import tpu as pltpu
from jax.sharding import Mesh, PartitionSpec as P

LEAF = 128
VMEM = 56 * 1024 * 1024
F32 = jnp.float32
BF16 = jnp.bfloat16
ALL = ("hi", "lo", "z", "core")


def split(value):
    high = value.astype(BF16)
    return high, (value - high.astype(F32)).astype(BF16)


def split_outside(value):
    high = lax.reduce_precision(value, exponent_bits=8, mantissa_bits=7)
    return high.astype(BF16), (value - high).astype(BF16)


def triple(left_high, left_low, right_high, right_low):
    dot = functools.partial(jnp.dot, preferred_element_type=F32)
    return dot(left_high, right_high) + (dot(left_high, right_low) + dot(left_low, right_high))


def swap(value, axis):
    return lax.ppermute(value, axis, [(0, 1), (1, 0)])


def shift(value, axis, step):
    count = lax.axis_size(axis)
    return lax.ppermute(value, axis, [(at, (at + step) % count) for at in range(count)])


def after(value, *others):
    return lax.optimization_barrier((value, others))[0]


def samples_kernel(place, front, test, out, test_high, test_low):
    step = pl.program_id(0)

    @pl.when(step == 0)
    def _():
        test_high[...], test_low[...] = split(test[...])

    rows, width = front.shape
    row_leaf = place[0] + step * (rows // LEAF) + lax.broadcasted_iota(jnp.int32, (rows, 1), 0) // LEAF
    col_leaf = place[1] + lax.broadcasted_iota(jnp.int32, (1, width), 1) // LEAF
    high, low = split(jnp.where(row_leaf == col_leaf, 0.0, front[...]))
    out[...] = triple(high, low, test_high[...], test_low[...])


def front_samples(place, front, test):
    height, width = front.shape
    samples = test.shape[1]
    rows = 512
    return pl.pallas_call(
        samples_kernel,
        out_shape=jax.ShapeDtypeStruct((height, samples), F32),
        grid_spec=pltpu.PrefetchScalarGridSpec(
            num_scalar_prefetch=1,
            grid=(height // rows,),
            in_specs=[
                pl.BlockSpec((rows, width), lambda s, place: (s, 0)),
                pl.BlockSpec((width, samples), lambda s, place: (0, 0), pipeline_mode=pl.Buffered(1)),
            ],
            out_specs=pl.BlockSpec((rows, samples), lambda s, place: (s, 0)),
            scratch_shapes=[pltpu.VMEM((width, samples), BF16)] * 2,
        ),
        compiler_params=pltpu.CompilerParams(vmem_limit_bytes=VMEM),
        cost_estimate=pl.CostEstimate(
            flops=6 * height * width * samples, bytes_accessed=height * width * 4, transcendentals=0
        ),
        name="samples",
    )(place, front, test)


def weights_kernel(parts, *refs):
    left_high, left_low, test = refs[:3]
    out_high, out_low, product_high, product_low, total = refs[3 + parts :]
    step = pl.program_id(0)
    high, low = split(jnp.concatenate([ref[...] for ref in refs[3 : 3 + parts]], axis=0))
    high, low = split(triple(left_high[...], left_low[...], high, low))
    out_high[...] = high
    out_low[...] = low
    part = triple(high, low, *split(test[...]))

    @pl.when(step == 0)
    def _():
        total[...] = part

    @pl.when(step > 0)
    def _():
        total[...] += part

    @pl.when(step == pl.num_programs(0) - 1)
    def _():
        product_high[...], product_low[...] = split(total[...])


def weights(left_high, left_low, test, blocks):
    panel = left_high.shape[0]
    width, samples = test.shape
    tile = min(width, 512)
    whole = pl.BlockSpec((panel, panel), lambda n: (0, 0), pipeline_mode=pl.Buffered(1))
    product = pl.BlockSpec((panel, samples), lambda n: (0, 0))
    return pl.pallas_call(
        functools.partial(weights_kernel, len(blocks)),
        out_shape=[jax.ShapeDtypeStruct((panel, width), BF16)] * 2 + [jax.ShapeDtypeStruct((panel, samples), BF16)] * 2,
        grid=(width // tile,),
        in_specs=[whole, whole, pl.BlockSpec((tile, samples), lambda n: (n, 0))]
        + [pl.BlockSpec((b.shape[0], tile), lambda n: (0, n)) for b in blocks],
        out_specs=[pl.BlockSpec((panel, tile), lambda n: (0, n))] * 2 + [product, product],
        scratch_shapes=[pltpu.VMEM((panel, samples), F32)],
        compiler_params=pltpu.CompilerParams(vmem_limit_bytes=VMEM),
        cost_estimate=pl.CostEstimate(
            flops=6 * panel * (panel + samples) * width, bytes_accessed=panel * width * 8, transcendentals=0
        ),
        name="weights",
    )(left_high, left_low, test, *blocks)


def terms_kernel(base, place, columns, partial, product_high, product_low, high, low, test, *refs):
    out, blocks = refs[-2:]
    slots, rows, _ = columns.shape
    left_high, left_low = split(jnp.concatenate([columns[at] for at in range(slots)], axis=1))
    out[...] = partial[...] - triple(left_high, left_low, product_high[...], product_low[...])
    tile = place[2] + base + pl.program_id(0)

    @pl.when((tile >= 0) & (tile < place[3]))
    def _():
        for at in range(rows // LEAF):
            piece = slice(at * LEAF, (at + 1) * LEAF)
            block = triple(left_high[piece], left_low[piece], high[:, piece], low[:, piece])
            out[piece] += triple(*split(block), *split(test[piece]))
            blocks[piece] = block


def terms(place, columns, partial, blocks, weight, product, test, start, tile):
    slots, rows, slot = columns.shape
    panel, width = weight[0].shape
    samples = test.shape[1]
    base = start // tile
    last = width // tile - 1

    def diagonal(i, place):
        return jnp.clip(place[2] + base + i, 0, last)

    whole = pl.BlockSpec((panel, samples), lambda i, place: (0, 0), pipeline_mode=pl.Buffered(1))
    strip = pl.BlockSpec((panel, tile), lambda i, place: (0, diagonal(i, place)))
    operands = [place, columns, partial, *product, *weight, test]
    specs = [
        pl.BlockSpec((slots, tile, slot), lambda i, place: (0, i, 0)),
        pl.BlockSpec((tile, samples), lambda i, place: (base + i, 0)),
        whole,
        whole,
        strip,
        strip,
        pl.BlockSpec((tile, samples), lambda i, place: (diagonal(i, place), 0)),
    ]
    aliases = {2: 0}
    if blocks is not None:
        aliases[len(operands)] = 1
        operands.append(blocks)
        specs.append(pl.BlockSpec(memory_space=pl.ANY))
    return pl.pallas_call(
        functools.partial(terms_kernel, base),
        out_shape=[
            jax.ShapeDtypeStruct(partial.shape, F32),
            jax.ShapeDtypeStruct((partial.shape[0], LEAF), F32),
        ],
        grid_spec=pltpu.PrefetchScalarGridSpec(
            num_scalar_prefetch=1,
            grid=(rows // tile,),
            in_specs=specs,
            out_specs=[
                pl.BlockSpec((tile, samples), lambda i, place: (base + i, 0)),
                pl.BlockSpec((tile, LEAF), lambda i, place: (base + i, 0)),
            ],
        ),
        input_output_aliases=aliases,
        compiler_params=pltpu.CompilerParams(vmem_limit_bytes=VMEM),
        cost_estimate=pl.CostEstimate(
            flops=6 * rows * panel * samples, bytes_accessed=rows * (panel + 2 * samples) * 4, transcendentals=0
        ),
        name="terms",
    )(*operands)


def leaves_kernel(place, front, blocks, out):
    for at in range(0, out.shape[0], LEAF):
        piece = slice(at, at + LEAF)
        out[piece] = front[piece, piece] - blocks[piece]


def leaf_blocks_here(place, front, blocks, tile):
    width = front.shape[1]
    return pl.pallas_call(
        leaves_kernel,
        out_shape=jax.ShapeDtypeStruct((width, LEAF), F32),
        grid_spec=pltpu.PrefetchScalarGridSpec(
            num_scalar_prefetch=1,
            grid=(width // tile,),
            in_specs=[
                pl.BlockSpec((tile, tile), lambda i, place: (place[4] + i, i)),
                pl.BlockSpec((tile, LEAF), lambda i, place: (place[4] + i, 0)),
            ],
            out_specs=pl.BlockSpec((tile, LEAF), lambda i, place: (i, 0)),
        ),
        compiler_params=pltpu.CompilerParams(vmem_limit_bytes=VMEM),
        cost_estimate=pl.CostEstimate(flops=width * LEAF, bytes_accessed=width * tile * 4, transcendentals=0),
        name="leaves",
    )(place, front, blocks)


def update_kernel(tiles, first, second, high, low, front, out):
    slots = first.shape[0]
    step = pl.program_id(0)
    columns = [jnp.where(step < tiles, first[at], second[at]) for at in range(slots)]
    left_high, left_low = split(jnp.concatenate(columns, axis=1))
    out[...] = front[...] - triple(left_high, left_low, high[...], low[...])


def update(chunks, weight, front):
    slots, _, slot = chunks[0].shape
    height, width = front.shape
    panel = weight[0].shape[0]
    tile = 256
    tiles = chunks[0].shape[1] // tile
    whole = pl.BlockSpec((panel, width), lambda i: (0, 0), pipeline_mode=pl.Buffered(1))
    return pl.pallas_call(
        functools.partial(update_kernel, tiles),
        out_shape=jax.ShapeDtypeStruct((height, width), F32),
        grid=(height // tile,),
        in_specs=[
            pl.BlockSpec((slots, tile, slot), lambda i: (0, jnp.minimum(i, tiles - 1), 0)),
            pl.BlockSpec((slots, tile, slot), lambda i: (0, jnp.maximum(i - tiles, 0), 0)),
            whole,
            whole,
            pl.BlockSpec((tile, width), lambda i: (i, 0)),
        ],
        out_specs=pl.BlockSpec((tile, width), lambda i: (i, 0)),
        compiler_params=pltpu.CompilerParams(vmem_limit_bytes=VMEM),
        cost_estimate=pl.CostEstimate(
            flops=6 * height * panel * width, bytes_accessed=height * width * 8 + panel * width * 4, transcendentals=0
        ),
        name="update",
    )(*chunks, *weight, front)


def chips_sum(value):
    chips, z = lax.axis_size("z"), lax.axis_index("z")
    parts = value.reshape(chips, value.shape[0] // chips, value.shape[1])
    total = lax.dynamic_index_in_dim(parts, z, 0, keepdims=False)
    for step in range(1, chips):
        part = lax.dynamic_index_in_dim(parts, (z + step) % chips, 0, keepdims=False)
        total = total + shift(part, "z", step)
    total = total + swap(total, "lo")
    parts = jnp.stack([total] + [shift(total, "z", step) for step in range(1, chips)])
    return jnp.take(parts, (z - jnp.arange(chips)) % chips, axis=0).reshape(value.shape)


def pack_kernel(core, rows, mine, other, blocks):
    high, low = split(rows[...])
    dot = functools.partial(
        lax.dot_general, dimension_numbers=(((0,), (0,)), ((), ())), preferred_element_type=F32
    )
    size = rows.shape[1]
    at = 0
    for start in range(0, size, LEAF):
        part, rest = slice(start, start + LEAF), slice(start, size)
        value = dot(high[:, part], high[:, rest]) + (dot(high[:, part], low[:, rest]) + dot(low[:, part], high[:, rest]))
        for column in range(0, size - start, LEAF):
            blocks[at : at + LEAF] = value[:, column : column + LEAF]
            at += LEAF
    half = at // 2
    first = core[0] == 0
    mine[...] = jnp.where(first, blocks[:half], blocks[half:])
    other[...] = jnp.where(first, blocks[half:], blocks[:half])


def packed_gram(core, rows):
    size = rows.shape[1]
    count = size // LEAF
    total = count * (count + 1) // 2 * LEAF
    return pl.pallas_call(
        pack_kernel,
        out_shape=[jax.ShapeDtypeStruct((total // 2, LEAF), F32)] * 2,
        in_specs=[pl.BlockSpec(memory_space=pltpu.SMEM), pl.BlockSpec(memory_space=pltpu.VMEM)],
        out_specs=[pl.BlockSpec(memory_space=pltpu.VMEM)] * 2,
        scratch_shapes=[pltpu.VMEM((total, LEAF), F32)],
        compiler_params=pltpu.CompilerParams(vmem_limit_bytes=VMEM),
        name="gram",
    )(core, rows)


def unpack_kernel(divisor, core, mine, other, out):
    size, half = out.shape[0], mine.shape[0]
    first = core[0] == 0
    at = 0
    for i in range(0, size, LEAF):
        for j in range(i, size, LEAF):
            low = at < half
            piece = slice(at % half, at % half + LEAF)
            block = jnp.where(first == low, mine[piece], other[piece]) / divisor
            out[i : i + LEAF, j : j + LEAF] = block
            if j > i:
                out[j : j + LEAF, i : i + LEAF] = block.T
            at += LEAF


def unpacked(core, mine, other, size, divisor):
    return pl.pallas_call(
        functools.partial(unpack_kernel, float(divisor)),
        out_shape=jax.ShapeDtypeStruct((size, size), F32),
        in_specs=[pl.BlockSpec(memory_space=pltpu.SMEM)] + [pl.BlockSpec(memory_space=pltpu.VMEM)] * 2,
        out_specs=pl.BlockSpec(memory_space=pltpu.VMEM),
        compiler_params=pltpu.CompilerParams(vmem_limit_bytes=VMEM),
        name="unpack",
    )(core, mine, other)


def leaves_to_rows(region, rows):
    row_count, chips = 2 * lax.axis_size("hi"), lax.axis_size("z")
    row, z = lax.axis_index("hi") * 2 + lax.axis_index("lo"), lax.axis_index("z")
    piece = 2 * rows // row_count
    half = chips // 2
    region = region.reshape(half, row_count, piece, LEAF)

    def part(step):
        return lax.dynamic_index_in_dim(region, (row + step) % row_count, 1, keepdims=False)

    share = jnp.where(row == z, part(0), 0.0)
    for step in range(1, row_count):
        route = []
        for r in range(row_count):
            for h in range(2):
                route.append(((r * chips + r) * 2 + h, ((r + step) % row_count * chips + r) * 2 + h))
        share = share + lax.ppermute(part(step), ALL, route)
    return share


def leaves_along(share):
    chips, z = lax.axis_size("z"), lax.axis_index("z")
    half = chips // 2
    received = []
    for turn in range(half):
        route = [
            (2 * at + h, 2 * (h * half + (at + turn) % half) + at // half) for at in range(chips) for h in range(2)
        ]
        sent = lax.dynamic_index_in_dim(share, (z + turn) % half, 0, keepdims=False)
        received.append(lax.ppermute(sent, ("z", "core"), route))
    return received


def leaves_across(received):
    row_count, chips = 2 * lax.axis_size("hi"), lax.axis_size("z")
    row, z = lax.axis_index("hi") * 2 + lax.axis_index("lo"), lax.axis_index("z")
    half = chips // 2
    stacked = jnp.stack(received)
    parts = []
    for turn in range(half):
        route = []
        for k in range(row_count):
            for at in range(chips):
                for e in range(2):
                    target = e * half + (turn + k) % half
                    route.append(((k * chips + at) * 2 + e, (target * chips + at) * 2 + k // half))
        which = (z - turn - row) % half
        parts.append(lax.ppermute(lax.dynamic_index_in_dim(stacked, which, 0, keepdims=False), ALL, route))
    stacked = jnp.stack(parts)
    ordered = [lax.dynamic_index_in_dim(stacked, (row - at) % half, 0, keepdims=False) for at in range(half)]
    return jnp.concatenate(ordered, axis=0)


def body(front_trailing, panel_columns, panel_rows, pivots, diag_inverse, test_matrix):
    hi_count, z_count = lax.axis_size("hi"), lax.axis_size("z")
    row_count, col_count = 2 * hi_count, 2 * z_count
    hi, lo, z, core = [lax.axis_index(name) for name in ALL]
    row, col = hi * 2 + lo, z * 2 + core
    height, width = front_trailing.shape
    depth = panel_rows.shape[0]
    panel = depth * row_count
    per = height // col_count
    tile = height // 8
    cut = height - tile
    place = jnp.stack(
        [
            row * (height // LEAF),
            col * (width // LEAF),
            row * (height // tile) - col * (width // tile),
            jnp.int32(width // tile),
            col % (col_count // row_count) * (width // tile),
        ]
    )

    first = lax.all_gather(panel_columns[:cut], ("z", "core"), axis=0, tiled=False)
    over_lo = swap(panel_rows, "lo")
    over_hi = [shift(panel_rows, "hi", step) for step in range(1, hi_count)]
    partial = front_samples(place, front_trailing, test_matrix)
    second = lax.all_gather(after(panel_columns[cut:], over_lo), ("z", "core"), axis=0, tiled=False)
    over_lo, *over_hi = after([over_lo, *over_hi], partial)
    blocks, owners = [panel_rows, over_lo], [row, row ^ 1]
    for step, block in enumerate(over_hi, 1):
        far_hi = (hi - step) % hi_count
        blocks += [block, shift(over_lo[: depth // 2], "hi", step), swap(block[depth // 2 :], "lo")]
        owners += [far_hi * 2 + lo, far_hi * 2 + (1 - lo)]

    position = (jnp.stack(owners)[:, None] * depth + jnp.arange(depth, dtype=jnp.int32)[None, :]).reshape(panel)
    chosen = (pivots[:, None] == position[None, :]).astype(BF16)
    left_high, left_low = [
        jnp.dot(part, chosen, preferred_element_type=F32).astype(BF16)
        for part in split_outside(after(diag_inverse, partial))
    ]
    high, low, *product = weights(left_high, left_low, test_matrix, blocks)

    weight = (high, low)
    partial, blocks = terms(place, first, partial, None, weight, product, test_matrix, 0, tile)
    small = tile // 2
    fine = place.at[2].set(row * (height // small) - col * (width // small)).at[3].set(width // small)
    partial, blocks = terms(fine, second, partial, blocks, weight, product, test_matrix, cut, small)
    off_samples = lax.psum_scatter(partial, ("z", "core"), scatter_dimension=0, tiled=True)

    leaves = leaf_blocks_here(place, front_trailing, blocks, tile)
    share = leaves_to_rows(leaves, per)
    received = leaves_along(share)
    schur = update((first, second), (after(high, partial, share), low), front_trailing)
    received = after(received, schur)
    leaf_blocks = leaves_across(received)
    cores = core.reshape(1)
    mine, other = packed_gram(cores, after(off_samples, leaf_blocks))
    mine = chips_sum(mine + swap(other, "core"))
    group_gram = unpacked(cores, mine, swap(mine, "core"), off_samples.shape[1], 2 * height)[None]
    return (schur, off_samples, leaf_blocks, group_gram)


def solution(mesh):
    rows, cols = mesh.shape["row"], mesh.shape["col"]
    fine = Mesh(mesh.devices.reshape(rows // 2, 2, cols // 2, 2), ALL)
    row, col = ("hi", "lo"), ("z", "core")
    placed = (P(row, col), P(row, col), P(row, col), P(), P(), P(col, None))
    return jax.shard_map(
        body,
        mesh=fine,
        in_specs=placed,
        out_specs=(P(row, col), P(ALL, None), P(ALL, None), P(row, None, None)),
        check_vma=False,
    )
```
